256 devices in a mesh: seq: 64 (over y, z, core), chan: 4 (over x).
Axes of the slice: x: 4, y: 4, z: 8, core: 2. Of those that a mesh axis runs over, the one named last changes fastest.
Arguments:
- query_proj: bfloat16 [16384, 4096], P('seq', 'chan'), may hold values from -6 to 6
- key_proj: bfloat16 [16384, 4096], P('seq', 'chan'), may hold values from -6 to 6
- value_proj: bfloat16 [16384, 4096], P('seq', 'chan'), may hold values from -6 to 6
- out_grad: bfloat16 [16384, 4096], P('seq', 'chan'), may hold values from -6 to 6
- residues: float32 [256, 16], replicated, may hold values from -2.1 to 2.1
- decay_rate: float32 [256, 16], replicated, as said below
- skip_gain: float32 [4096], P('chan'), may hold values from -3 to 3
Outputs:
- layer_out: bfloat16 [16384, 4096], P('seq', 'chan')
- key_grad: bfloat16 [16384, 4096], P('seq', 'chan')
- value_grad: bfloat16 [16384, 4096], P('seq', 'chan')
- filter_grad: float32 [16384, 256], P('seq', 'chan')
The draws below stay inside these ranges and needn't reach their ends.
Inputs may be any that keep to these rules, and one draw needn't show every extreme that they name: `decay_rate`: every rate is positive.
All inputs are finite; a program needn't handle non-finite values.
Results may differ from the reference program's by a relative error of at most 0.022.
Values may be sent and summed in bfloat16 or wider, within the bound.
A program may use at most 192 MiB of HBM per device.

```python
import math
import jax
import jax.numpy as jnp
from jax import lax

CHANNELS = 4096
FILTERS = 256
MODES = 16
SEQ_LEN = 16384


def draw_decay_rate(key, part):
    pick_key, slow_key, fast_key = jax.random.split(key, 3)
    slow_share = 0.5
    slow_low = 0.25 / SEQ_LEN
    slow_high = 2.0 / SEQ_LEN
    grid_shape = (FILTERS, MODES)
    slow_pick = jax.random.bernoulli(pick_key, slow_share, grid_shape)
    slow_rates = jnp.exp(jax.random.uniform(slow_key, grid_shape, jnp.float32, math.log(slow_low), math.log(slow_high)))
    fast_rates = jnp.exp(jax.random.uniform(fast_key, grid_shape, jnp.float32, math.log(1.0 / 50.0), math.log(1.0 / 20.0)))
    return jnp.where(slow_pick, slow_rates, fast_rates).astype(jnp.float32)


def steps_of(stream_key, dims, cuts, smallest, top_value):
    level = 1.0
    for axis_at, blocks in cuts:
        heights = jax.random.uniform(jax.random.fold_in(jax.random.fold_in(stream_key, 6), axis_at), (blocks,), jnp.float32, smallest / len(cuts), top_value / len(cuts))
        level = level * jnp.repeat(jnp.exp(heights), dims[axis_at] // blocks).reshape((-1,) + (1,) * (len(dims) - 1 - axis_at))
    return level


def centred(own_key, extent, width, reach, cuts=(), kind=jnp.bfloat16):
    entries = width * jax.random.normal(own_key, extent, jnp.float32)
    if cuts:
        entries = entries * steps_of(own_key, extent, cuts, -0.22, 0.18)
    return jnp.clip(entries, -reach, reach).astype(kind)


def setup_inputs(seed: int = 0) -> dict:
    streams_of = jax.random.split(jax.random.key(seed), 8)
    return {
        "query_proj": centred(streams_of[0], (SEQ_LEN, CHANNELS), 1.0, 6.0, ((0, 64), (1, 4))),
        "key_proj": centred(streams_of[1], (SEQ_LEN, CHANNELS), 1.0, 6.0, ((0, 64), (1, 4))),
        "value_proj": centred(streams_of[2], (SEQ_LEN, CHANNELS), 1.0, 6.0, ((0, 64), (1, 4))),
        "out_grad": centred(streams_of[3], (SEQ_LEN, CHANNELS), 1.0, 6.0, ((0, 64), (1, 4))),
        "residues": centred(streams_of[4], (FILTERS, MODES), 0.35, 2.1, (), jnp.float32),
        "decay_rate": draw_decay_rate(jax.random.fold_in(streams_of[7], 71), 0),
        "skip_gain": centred(streams_of[6], (CHANNELS,), 0.5, 3.0, ((0, 4),), jnp.float32),
    }


def filter_taps(residues, decay_rate, positions):
    weight = residues * jnp.sqrt(decay_rate)

    def one_filter(row_pair):
        weight_row, rate_row = row_pair
        return lax.optimization_barrier(jnp.sum(weight_row[:, None] * jnp.exp(-(rate_row[:, None] * positions[None, :])), axis=0))
    return lax.map(one_filter, (weight, decay_rate))

def reference(query_proj, key_proj, value_proj, out_grad, residues, decay_rate, skip_gain):
    length = SEQ_LEN
    fft_size = 2 * length
    blocks = CHANNELS // FILTERS
    conv_in = (key_proj.astype(jnp.float32) * value_proj.astype(jnp.float32)).astype(jnp.bfloat16)
    mid_grad = (out_grad.astype(jnp.float32) * query_proj.astype(jnp.float32)).astype(jnp.bfloat16)
    positions = jnp.arange(length, dtype=jnp.int32).astype(jnp.float32)
    taps = filter_taps(residues, decay_rate, positions)
    spectrum = jnp.fft.fft(taps, n=fft_size, axis=1).T

    def block_step(totals, block_id):
        first_col = (block_id * FILTERS).astype(jnp.int32)

        def columns(source):
            return lax.dynamic_slice_in_dim(source, first_col, FILTERS, 1).astype(jnp.float32)
        conv_block = columns(conv_in)
        grad_block = columns(mid_grad)
        query_block = columns(query_proj)
        key_block = columns(key_proj)
        value_block = columns(value_proj)
        gain_block = lax.dynamic_slice_in_dim(skip_gain, first_col, FILTERS, 0)[None, :]
        conv_spec = jnp.fft.fft(conv_block, n=fft_size, axis=0)
        grad_spec = jnp.fft.fft(grad_block, n=fft_size, axis=0)
        long_conv = jnp.fft.ifft(spectrum * conv_spec, axis=0)[:length].real
        corr_part = jnp.fft.ifft(jnp.conj(spectrum) * grad_spec, axis=0)[:length].real
        product = jnp.conj(conv_spec) * grad_spec
        totals = (totals[0] + product.real, totals[1] + product.imag)
        layer_block = (query_block * (long_conv + gain_block * conv_block)).astype(jnp.bfloat16)
        total_grad = corr_part + gain_block * grad_block
        key_block_grad = (total_grad * value_block).astype(jnp.bfloat16)
        value_block_grad = (total_grad * key_block).astype(jnp.bfloat16)
        return (totals, (layer_block, key_block_grad, value_block_grad))
    zero_sum = jnp.zeros((fft_size, FILTERS), jnp.float32)
    totals, outputs = lax.scan(block_step, (zero_sum, zero_sum), jnp.arange(blocks, dtype=jnp.int32))

    def assemble(stacked):
        return jnp.transpose(stacked, (1, 0, 2)).reshape(length, CHANNELS)
    scale = 1.0 / math.sqrt(SEQ_LEN * (CHANNELS // FILTERS))
    filter_grad = (jnp.fft.ifft(totals[0] + 1j * totals[1], axis=0)[:length].real * scale).astype(jnp.float32)
    return (assemble(outputs[0]), assemble(outputs[1]), assemble(outputs[2]), filter_grad)
```

```python
import math

import jax
import jax.numpy as jnp
from jax import lax
from jax.experimental import pallas as pl
from jax.experimental.pallas import tpu as pltpu
from jax.sharding import PartitionSpec as P

CHANNELS = 4096
FILTERS = 256
MODES = 16
SEQ_LEN = 16384
SHARDS = 64
ROWS = 256
GROUPS = 4
F32 = jnp.float32
BF16 = jnp.bfloat16
LANES = 128
STEPS = 32
SUBS = 8
TILES = 8
ACROSS = (((1,), (1,)), ((), ()))


def iota(shape, dim):
    return lax.broadcasted_iota(jnp.int32, shape, dim)


def identity(size):
    return (iota((size, size), 0) == iota((size, size), 1)).astype(BF16)


def reversal(size):
    row, col = iota((size, size), 0), iota((size, size), 1)
    return ((row + col == size) | ((row == 0) & (col == 0))).astype(BF16)


def load_signals(q_ref, k_ref, v_ref, o_ref, sig_ref):
    for tile in range(TILES):
        lanes = pl.ds(tile * LANES, LANES)
        conv_in = (k_ref[:, lanes].astype(F32) * v_ref[:, lanes].astype(F32)).astype(BF16)
        mid_grad = (o_ref[:, lanes].astype(F32) * q_ref[:, lanes].astype(F32)).astype(BF16)
        sig_ref[0, tile] = conv_in.astype(F32)
        sig_ref[1, tile] = mid_grad.astype(F32)


def pack_chunk(chunk, sig_ref, spread_ref, pack_ref):
    eye = identity(LANES)
    rev = reversal(LANES)
    for group in range(GROUPS):
        tile = 2 * group + chunk
        for sig in range(2):
            for half in range(2):
                block = sig_ref[sig, tile, half * LANES:(half + 1) * LANES, :].astype(BF16)
                if sig == 0:
                    block = jnp.dot(rev, block, preferred_element_type=F32).astype(BF16)
                turned = lax.dot_general(eye, block, ACROSS, preferred_element_type=F32)
                for low in range(2):
                    place = sig * 8 + low * 4 + group
                    spread_ref[half, pl.ds(place, SHARDS, stride=16), :] = turned[
                        low * SHARDS:(low + 1) * SHARDS
                    ]
    for half in range(2):
        pack_ref[chunk, :, half * LANES:(half + 1) * LANES] = spread_ref[half].astype(BF16)


def make_decays(rates_ref, weights_ref, base_ref, gain_ref):
    for side in range(2):
        for mode in range(MODES):
            rate = jnp.broadcast_to(rates_ref[side, mode:mode + 1, :], (SUBS, LANES))
            base_ref[side, mode] = jnp.exp(-rate)
            gain_ref[side, mode] = jnp.broadcast_to(
                weights_ref[side, mode:mode + 1, :], (SUBS, LANES)
            ) * jnp.sqrt(rate)


def block_states(sig_ref, rates_ref, base_ref, ends_ref, state_ref):
    sub = iota((SUBS, LANES), 0).astype(F32)

    def one_group(group, _):
        for side in range(2):
            tile = 2 * group + side
            base = [base_ref[side, mode] for mode in range(MODES)]
            for sig in range(2):
                acc = None
                for step in range(STEPS):
                    place = step if sig == 0 else STEPS - 1 - step
                    row = sig_ref[sig, tile, pl.ds(place, SUBS, stride=STEPS), :]
                    if acc is None:
                        acc = [row] * MODES
                    else:
                        acc = [b * a + row for b, a in zip(base, acc)]
                steps_left = (SUBS - 1.0 - sub if sig == 0 else sub) * float(STEPS)
                for mode in range(MODES):
                    ends_ref[sig, tile, mode] = acc[mode]
                    rate = rates_ref[side, mode:mode + 1, :]
                    whole = jnp.sum(acc[mode] * jnp.exp(-rate * steps_left), axis=0, keepdims=True)
                    state_ref[mode * GROUPS + group, sig * 2 + side:sig * 2 + side + 1, :] = whole
        return _
    lax.fori_loop(0, GROUPS, one_group, 0)


def scan_blocks(mode, rates_ref, got_ref, enter_ref):
    decay = [
        jnp.exp(-float(ROWS) * rates_ref[side, pl.ds(mode, 1), :]) for side in range(2)
    ]

    def step(at, held):
        back = SHARDS - 1 - at
        out = []
        for sig in range(2):
            place = at if sig == 0 else back
            for side in range(2):
                now = held[sig * 2 + side]
                rows = slice(sig * 2 + side, sig * 2 + side + 1)
                enter_ref[place, rows, :] = now
                out.append(decay[side] * now + got_ref[place, rows, :])
        return tuple(out)
    lax.fori_loop(0, SHARDS, step, (jnp.zeros((1, LANES), F32),) * 4)


def run_recurrence(sig_ref, rates_ref, base_ref, gain_ref, ends_ref, enter_ref, long_ref):
    sub = iota((SUBS, LANES), 0)

    def one_group(group, _):
        for side in range(2):
            tile = 2 * group + side
            base = [base_ref[side, mode] for mode in range(MODES)]
            gain = [gain_ref[side, mode] for mode in range(MODES)]
            for sig in range(2):
                held = []
                for mode in range(MODES):
                    rate = rates_ref[side, mode:mode + 1, :]
                    first = enter_ref[mode * GROUPS + group, sig * 2 + side:sig * 2 + side + 1, :]
                    ends = ends_ref[sig, tile, mode]
                    if sig == 0:
                        state = jnp.where(sub == 0, first, pltpu.roll(ends, 1, 0))
                    else:
                        state = jnp.where(sub == SUBS - 1, first, pltpu.roll(ends, SUBS - 1, 0))
                    for hop in (1, 2, 4):
                        decay = jnp.exp(-float(STEPS * hop) * rate)
                        if sig == 0:
                            moved = jnp.where(sub >= hop, pltpu.roll(state, hop, 0), 0.0)
                        else:
                            moved = jnp.where(sub < SUBS - hop, pltpu.roll(state, SUBS - hop, 0), 0.0)
                        state = state + decay * moved
                    held.append(state)
                for step in range(STEPS):
                    place = step if sig == 0 else STEPS - 1 - step
                    where = pl.ds(place, SUBS, stride=STEPS)
                    row = sig_ref[sig, tile, where, :]
                    held = [b * h + row for b, h in zip(base, held)]
                    terms = [w * h for w, h in zip(gain, held)]
                    while len(terms) > 1:
                        terms = [a + b for a, b in zip(terms[::2], terms[1::2])]
                    long_ref[sig, tile, where, :] = terms[0]
        return _
    lax.fori_loop(0, GROUPS, one_group, 0)


def finish_outputs(q_ref, k_ref, v_ref, skip_ref, sig_ref, long_ref, layer_ref, kgrad_ref, vgrad_ref):
    for tile in range(TILES):
        lanes = pl.ds(tile * LANES, LANES)
        skip = skip_ref[:, lanes]
        layer = long_ref[0, tile] + skip * sig_ref[0, tile]
        layer_ref[:, lanes] = (q_ref[:, lanes].astype(F32) * layer).astype(BF16)
        total = long_ref[1, tile] + skip * sig_ref[1, tile]
        kgrad_ref[:, lanes] = (total * v_ref[:, lanes].astype(F32)).astype(BF16)
        vgrad_ref[:, lanes] = (total * k_ref[:, lanes].astype(F32)).astype(BF16)


PAD = ROWS
WINDOW = 528


def correlate_filter(chunk, low, got_ref, rows_ref, slide_ref, slid_ref, grad_ref, turn_ref, keep_ref, sums_ref, out_ref):
    eye = identity(ROWS)
    for half in range(2):
        lanes = slice(half * LANES, (half + 1) * LANES)
        for group in range(GROUPS):
            conv_rows = rows_ref[half, pl.ds(low * 4 + group, SHARDS, stride=16), :]
            for early in range(4):
                slide_ref[early, half, pl.ds(PAD + group + 4 * early, SHARDS, stride=4), :] = conv_rows
            grad_ref[half, pl.ds(group, SHARDS, stride=4), :] = rows_ref[
                half, pl.ds(8 + low * 4 + group, SHARDS, stride=16), :
            ]
        for early in range(4):
            slid_ref[early, :, lanes] = slide_ref[early, half, :2 * ROWS, :].astype(BF16)
        turn_ref[lanes, :] = lax.dot_general(
            identity(LANES), grad_ref[half].astype(BF16), ACROSS, preferred_element_type=F32
        ).astype(BF16)

    row, lane = iota((LANES, LANES), 0), iota((LANES, LANES), 1)
    causal = (lane == 0) | (row + lane >= LANES)
    turn = turn_ref[...]
    keep_ref[...] = jnp.zeros_like(keep_ref)

    def sheared(block):
        total = block[:SUBS]
        for part in range(1, LANES // SUBS):
            total = total + pltpu.roll(block[part * SUBS:(part + 1) * SUBS], part * SUBS, 1)
        return total

    def four_lags(at, _):
        far = SHARDS // 4 - 1 - at
        for early in (3, 2, 1, 0):
            start = pl.multiple_of(PAD - 16 * far, 16)
            window = slid_ref[early, pl.ds(start, ROWS), :]
            prod = jnp.dot(turn, window, preferred_element_type=F32)
            odd = prod[LANES:, :LANES] + keep_ref[0]
            even = prod[:LANES, :LANES] + prod[LANES:, LANES:]
            odd_row = jnp.where(causal, odd, keep_ref[1])
            even_row = jnp.where(causal, even, odd)
            keep_ref[0] = prod[:LANES, LANES:]
            keep_ref[1] = even
            sums_ref[4 * far + early, 0] = sheared(even_row)
            sums_ref[4 * far + early, 1] = sheared(odd_row)
        return _
    lax.fori_loop(0, SHARDS // 4, four_lags, 0)

    def gather(at, _):
        for part in range(2):
            block = pltpu.roll(sums_ref[at, part], 0, 1, stride=1, stride_axis=0)
            out_ref[2 * chunk + low, at, part:part + 1, :] = jnp.sum(block, axis=0, keepdims=True)
        return _
    lax.fori_loop(0, SHARDS, gather, 0)


def prep_kernel(q_ref, k_ref, v_ref, o_ref, rates_ref, weights_ref, pack_ref, state_ref, ends_ref,
                sig_ref, spread_ref, base_ref, gain_ref):
    load_signals(q_ref, k_ref, v_ref, o_ref, sig_ref)
    for chunk in range(2):
        pack_chunk(chunk, sig_ref, spread_ref, pack_ref)
    make_decays(rates_ref, weights_ref, base_ref, gain_ref)
    block_states(sig_ref, rates_ref, base_ref, ends_ref, state_ref)


def scan_kernel(rates_ref, got_ref, enter_ref):
    mode = lax.axis_index("seq") // GROUPS
    scan_blocks(mode, rates_ref, got_ref, enter_ref)


def output_kernel(q_ref, k_ref, v_ref, o_ref, rates_ref, weights_ref, skip_ref, ends_ref, enter_ref,
                  layer_ref, kgrad_ref, vgrad_ref, sig_ref, base_ref, gain_ref, long_ref):
    load_signals(q_ref, k_ref, v_ref, o_ref, sig_ref)
    make_decays(rates_ref, weights_ref, base_ref, gain_ref)
    run_recurrence(sig_ref, rates_ref, base_ref, gain_ref, ends_ref, enter_ref, long_ref)
    finish_outputs(q_ref, k_ref, v_ref, skip_ref, sig_ref, long_ref, layer_ref, kgrad_ref, vgrad_ref)


def correlate_kernel(got_ref, out_ref, rows_ref, slide_ref, slid_ref, grad_ref, turn_ref, keep_ref, sums_ref):
    slide_ref[...] = jnp.zeros_like(slide_ref)
    for chunk in range(2):
        for half in range(2):
            rows_ref[half] = got_ref[chunk, :, half * LANES:(half + 1) * LANES].astype(F32)
        for low in range(2):
            correlate_filter(
                chunk, low, got_ref, rows_ref, slide_ref, slid_ref, grad_ref, turn_ref, keep_ref, sums_ref, out_ref
            )


CORRELATE_SCRATCH = [
    pltpu.VMEM((2, SHARDS * 16, LANES), F32),
    pltpu.VMEM((4, 2, WINDOW, LANES), F32),
    pltpu.VMEM((4, 2 * ROWS, ROWS), BF16),
    pltpu.VMEM((2, ROWS, LANES), F32),
    pltpu.VMEM((ROWS, ROWS), BF16),
    pltpu.VMEM((2, LANES, LANES), F32),
    pltpu.VMEM((SHARDS, 2, SUBS, LANES), F32),
]
SIGNALS = pltpu.VMEM((2, TILES, ROWS, LANES), F32)
DECAYS = pltpu.VMEM((2, MODES, SUBS, LANES), F32)
VMEM = pl.BlockSpec(memory_space=pltpu.VMEM)


def call(kernel, shapes, scratch, count):
    return pl.pallas_call(
        kernel,
        out_shape=shapes,
        in_specs=[VMEM] * count,
        out_specs=jax.tree.map(lambda _: VMEM, shapes),
        scratch_shapes=scratch,
        compiler_params=pltpu.CompilerParams(vmem_limit_bytes=56 * 2**20),
    )


def per_device(query_proj, key_proj, value_proj, out_grad, residues, decay_rate, skip_gain):
    sds = jax.ShapeDtypeStruct
    rates = decay_rate.reshape(2, LANES, MODES).transpose(0, 2, 1)
    weights = residues.reshape(2, LANES, MODES).transpose(0, 2, 1)
    pack, state, ends = call(
        prep_kernel,
        (sds((2, SHARDS * 16, ROWS), BF16), sds((SHARDS, 4, LANES), F32), sds((2, TILES, MODES, SUBS, LANES), F32)),
        [SIGNALS, pltpu.VMEM((2, SHARDS * 16, LANES), F32), DECAYS, DECAYS],
        6,
    )(query_proj, key_proj, value_proj, out_grad, rates, weights)
    got = lax.all_to_all(state, "seq", split_axis=0, concat_axis=0, tiled=True)
    arrived = lax.all_to_all(
        pack.reshape(2, SHARDS, 16, ROWS), "seq", split_axis=1, concat_axis=1, tiled=True
    ).reshape(2, SHARDS * 16, ROWS)
    enter = call(scan_kernel, sds((SHARDS, 4, LANES), F32), [], 2)(rates, got)
    enter = lax.all_to_all(enter, "seq", split_axis=0, concat_axis=0, tiled=True)
    layer, kgrad, vgrad = call(
        output_kernel,
        (sds((ROWS, 1024), BF16),) * 3,
        [SIGNALS, DECAYS, DECAYS, SIGNALS],
        9,
    )(query_proj, key_proj, value_proj, out_grad, rates, weights, skip_gain[None, :], ends, enter)
    shares = call(correlate_kernel, sds((4, SHARDS, 2, LANES), F32), CORRELATE_SCRATCH, 1)(arrived)
    shares = lax.all_to_all(shares, "chan", split_axis=0, concat_axis=0, tiled=True)
    taps = shares.sum(axis=0)
    taps = lax.all_to_all(taps, "seq", split_axis=0, concat_axis=0, tiled=True)
    scale = 1.0 / math.sqrt(SEQ_LEN * (CHANNELS // FILTERS))
    filter_grad = taps.reshape(SHARDS, ROWS).T * scale
    return (layer, kgrad, vgrad, filter_grad)


def solution(mesh):
    wide = P("seq", "chan")
    return jax.shard_map(
        per_device,
        mesh=mesh,
        in_specs=(wide, wide, wide, wide, P(), P(), P("chan")),
        out_specs=(wide, wide, wide, wide),
        check_vma=False,
    )
```

```python
import math

import jax
import jax.numpy as jnp
from jax import lax
from jax.experimental import pallas as pl
from jax.experimental.pallas import tpu as pltpu
from jax.sharding import PartitionSpec as P

CHANNELS = 4096
FILTERS = 256
MODES = 16
SEQ_LEN = 16384
SHARDS = 64
ROWS = 256
GROUPS = 4
F32 = jnp.float32
BF16 = jnp.bfloat16
LANES = 128
STEPS = 32
WORKERS = 16
SUBS = 8
TILES = 8
ACROSS = (((1,), (1,)), ((), ()))


def iota(shape, dim):
    return lax.broadcasted_iota(jnp.int32, shape, dim)


def identity(size):
    return (iota((size, size), 0) == iota((size, size), 1)).astype(BF16)


def reversal(size):
    row, col = iota((size, size), 0), iota((size, size), 1)
    return ((row + col == size) | ((row == 0) & (col == 0))).astype(BF16)


def load_signals(q_ref, k_ref, v_ref, o_ref, sig_ref):
    for tile in range(TILES):
        lanes = pl.ds(tile * LANES, LANES)
        conv_in = (k_ref[:, lanes].astype(F32) * v_ref[:, lanes].astype(F32)).astype(BF16)
        mid_grad = (o_ref[:, lanes].astype(F32) * q_ref[:, lanes].astype(F32)).astype(BF16)
        sig_ref[0, tile] = conv_in.astype(F32)
        sig_ref[1, tile] = mid_grad.astype(F32)


def pack_chunk(chunk, sig_ref, spread_ref, pack_ref):
    eye = identity(LANES)
    rev = reversal(LANES)
    for group in range(GROUPS):
        tile = 2 * group + chunk
        for sig in range(2):
            for half in range(2):
                block = sig_ref[sig, tile, half * LANES:(half + 1) * LANES, :].astype(BF16)
                if sig == 0:
                    block = jnp.dot(rev, block, preferred_element_type=F32).astype(BF16)
                turned = lax.dot_general(eye, block, ACROSS, preferred_element_type=F32)
                for low in range(2):
                    place = sig * 8 + low * 4 + group
                    spread_ref[half, pl.ds(place, SHARDS, stride=16), :] = turned[
                        low * SHARDS:(low + 1) * SHARDS
                    ]
    for half in range(2):
        pack_ref[chunk, :, half * LANES:(half + 1) * LANES] = spread_ref[half].astype(BF16)


def make_decays(rates_ref, weights_ref, base_ref, gain_ref, leave_ref, hop_ref):
    sub = iota((MODES, SUBS, LANES), 1)
    for side in range(2):
        lanes = slice(side * LANES, (side + 1) * LANES)
        rate = jnp.broadcast_to(rates_ref[:, lanes][:, None, :], (MODES, SUBS, LANES))
        weight = jnp.broadcast_to(weights_ref[:, lanes][:, None, :], (MODES, SUBS, LANES))
        base_ref[side] = jnp.exp(-rate)
        gain_ref[side] = weight * jnp.sqrt(rate)
        for sig in range(2):
            runs = SUBS - 1 - sub if sig == 0 else sub
            leave_ref[sig, side] = jnp.exp(-rate * (runs.astype(F32) * float(STEPS)))
            for at, hop in enumerate((1, 2, 4)):
                left = sub >= hop if sig == 0 else sub < SUBS - hop
                hop_ref[sig, side, at] = jnp.where(left, jnp.exp(-rate * float(STEPS * hop)), 0.0)


def block_states(sig_ref, base_ref, leave_ref, ends_ref, state_ref, state_out):
    def one_group(group, _):
        for side in range(2):
            tile = 2 * group + side
            base = base_ref[side]
            for sig in range(2):
                acc = None
                for step in range(STEPS):
                    place = step if sig == 0 else STEPS - 1 - step
                    row = sig_ref[sig, tile, pl.ds(place, SUBS, stride=STEPS), :]
                    wide = jnp.broadcast_to(row[None], (MODES, SUBS, LANES))
                    acc = wide if acc is None else base * acc + wide
                ends_ref[sig, tile] = acc
                start = pl.multiple_of((sig * TILES + tile) * MODES, MODES)
                state_ref[pl.ds(start, MODES), :] = jnp.sum(acc * leave_ref[sig, side], axis=1)
        return _
    lax.fori_loop(0, GROUPS, one_group, 0)
    for mode in range(MODES):
        state_out[mode] = state_ref[pl.ds(mode, 2 * TILES, stride=MODES), :].astype(BF16)


def owner_scan(decay, got_ref, first, enter_ref):
    fore, back = first
    for at in range(WORKERS):
        far = WORKERS - 1 - at
        if enter_ref is not None:
            enter_ref[at, :TILES, :] = fore
            enter_ref[far, TILES:, :] = back
        fore = decay * fore + got_ref[at, :, :].astype(F32)[:TILES]
        back = decay * back + got_ref[far, :, :].astype(F32)[TILES:]
    return fore, back


def run_recurrence(sig_ref, base_ref, gain_ref, hop_ref, ends_ref, enter_ref, long_ref):
    sub = iota((MODES, SUBS, LANES), 1)

    def one_group(group, _):
        for side in range(2):
            tile = 2 * group + side
            base, gain = base_ref[side], gain_ref[side]
            for sig in range(2):
                first = jnp.broadcast_to(enter_ref[sig * TILES + tile][:, None, :], (MODES, SUBS, LANES))
                ends = ends_ref[sig, tile]
                edge, turn = (0, 1) if sig == 0 else (SUBS - 1, SUBS - 1)
                held = jnp.where(sub == edge, first, pltpu.roll(ends, turn, 1))
                for at, hop in enumerate((1, 2, 4)):
                    moved = pltpu.roll(held, hop if sig == 0 else SUBS - hop, 1)
                    held = held + hop_ref[sig, side, at] * moved
                for step in range(STEPS):
                    place = step if sig == 0 else STEPS - 1 - step
                    where = pl.ds(place, SUBS, stride=STEPS)
                    row = sig_ref[sig, tile, where, :]
                    held = base * held + jnp.broadcast_to(row[None], (MODES, SUBS, LANES))
                    terms = gain * held
                    for width in (8, 4, 2, 1):
                        terms = terms[:width] + terms[width:]
                    long_ref[sig, tile, where, :] = terms[0]
        return _
    lax.fori_loop(0, GROUPS, one_group, 0)


def finish_outputs(q_ref, k_ref, v_ref, skip_ref, sig_ref, long_ref, layer_ref, kgrad_ref, vgrad_ref):
    for tile in range(TILES):
        lanes = pl.ds(tile * LANES, LANES)
        skip = skip_ref[:, lanes]
        layer = long_ref[0, tile] + skip * sig_ref[0, tile]
        layer_ref[:, lanes] = (q_ref[:, lanes].astype(F32) * layer).astype(BF16)
        total = long_ref[1, tile] + skip * sig_ref[1, tile]
        kgrad_ref[:, lanes] = (total * v_ref[:, lanes].astype(F32)).astype(BF16)
        vgrad_ref[:, lanes] = (total * k_ref[:, lanes].astype(F32)).astype(BF16)


PAD = ROWS
WINDOW = 528
LONG = 4


def correlate_filter(low, rows_ref, slide_ref, slid_ref, grad_ref, turn_ref, keep_ref, sums_ref):
    for half in range(2):
        lanes = slice(half * LANES, (half + 1) * LANES)
        for group in range(GROUPS):
            conv_rows = rows_ref[half, pl.ds(low * 4 + group, SHARDS, stride=16), :]
            for early in range(4):
                slide_ref[early, half, pl.ds(PAD + group + 4 * early, SHARDS, stride=4), :] = conv_rows
            grad_ref[half, pl.ds(group, SHARDS, stride=4), :] = rows_ref[
                half, pl.ds(8 + low * 4 + group, SHARDS, stride=16), :
            ]
        for early in range(4):
            slid_ref[early, :, lanes] = slide_ref[early, half, :2 * ROWS, :].astype(BF16)
        turn_ref[lanes, :] = lax.dot_general(
            identity(LANES), grad_ref[half].astype(BF16), ACROSS, preferred_element_type=F32
        ).astype(BF16)

    row, lane = iota((LANES, LANES), 0), iota((LANES, LANES), 1)
    causal = (lane == 0) | (row + lane >= LANES)
    turn = turn_ref[...]
    keep_ref[...] = jnp.zeros_like(keep_ref)

    def sheared(block):
        block = pltpu.roll(block, 0, 1, stride=1, stride_axis=0)
        return jnp.sum(block.reshape(LANES // SUBS, SUBS, LANES), axis=0)

    def some_lags(at, _):
        corner, later = keep_ref[0], keep_ref[1]
        for inner in range(LONG):
            far = SHARDS // 4 - 1 - (at * LONG + inner)
            for early in (3, 2, 1, 0):
                start = pl.multiple_of(PAD - 16 * far, 16)
                window = slid_ref[early, pl.ds(start, ROWS), :]
                prod = jnp.dot(turn, window, preferred_element_type=F32)
                odd = prod[LANES:, :LANES] + corner
                even = prod[:LANES, :LANES] + prod[LANES:, LANES:]
                place = pl.multiple_of((4 * far + early) * 2 * SUBS, 2 * SUBS)
                sums_ref[pl.ds(place, SUBS), :] = sheared(jnp.where(causal, even, odd))
                sums_ref[pl.ds(place + SUBS, SUBS), :] = sheared(jnp.where(causal, odd, later))
                corner, later = prod[:LANES, LANES:], even
        keep_ref[0], keep_ref[1] = corner, later
        return _
    lax.fori_loop(0, SHARDS // 4 // LONG, some_lags, 0)

    out = []
    for part in range(2):
        total = sums_ref[pl.ds(part * SUBS, SHARDS, stride=2 * SUBS), :]
        for sub in range(1, SUBS):
            total = total + sums_ref[pl.ds(part * SUBS + sub, SHARDS, stride=2 * SUBS), :]
        out.append(total)
    return jnp.concatenate(out, axis=0)


def seq_copy(src, dst, send, recv, to):
    return pltpu.make_async_remote_copy(
        src_ref=src, dst_ref=dst, send_sem=send, recv_sem=recv,
        device_id={"seq": to}, device_id_type=pl.DeviceIdType.MESH,
    )


def settle(ref, sem):
    pltpu.make_async_copy(ref, ref, sem).wait()


def layer_kernel(q_ref, k_ref, v_ref, o_ref, rates_ref, weights_ref, skip_ref,
                 layer_ref, kgrad_ref, vgrad_ref, taps_ref,
                 sig_ref, spread_ref, pack_ref, land_ref, base_ref, gain_ref, leave_ref, hop_ref, ends_ref,
                 state_ref, left_ref, got_ref, whole_ref, wholes_ref, enter_ref, given_ref, entered_ref, first_ref,
                 long_ref, rows_ref, slide_ref, slid_ref, grad_ref, turn_ref, keep_ref, sums_ref,
                 share_ref, sent_ref, came_ref, final_ref, home_ref, send_sem, recv_sem, own_sem):
    seq, chan = lax.axis_index("seq"), lax.axis_index("chan")
    row, worker = lax.div(seq, WORKERS), lax.rem(seq, WORKERS)
    barrier = pltpu.get_barrier_semaphore()

    def greet(step, _):
        pl.semaphore_signal(barrier, inc=1, device_id={"seq": lax.rem(seq + step, SHARDS)}, device_id_type=pl.DeviceIdType.MESH)
        return _
    lax.fori_loop(1, SHARDS, greet, 0)
    for step in range(1, 4):
        pl.semaphore_signal(barrier, inc=1, device_id={"chan": lax.rem(chan + step, 4)}, device_id_type=pl.DeviceIdType.MESH)

    load_signals(q_ref, k_ref, v_ref, o_ref, sig_ref)

    own_copies = []

    def send_chunk(chunk):
        mine = pl.ds(pl.multiple_of(seq * 16, 16), 16)
        own = pltpu.make_async_copy(pack_ref.at[chunk, mine], land_ref.at[chunk, mine], own_sem.at[chunk])
        own.start()
        own_copies.append(own)

        def one(step, _):
            to = lax.rem(seq + step, SHARDS)
            seq_copy(
                pack_ref.at[chunk, pl.ds(pl.multiple_of(to * 16, 16), 16)], land_ref.at[chunk, mine],
                send_sem.at[chunk], recv_sem.at[chunk], to,
            ).start()
            return _
        lax.fori_loop(1, SHARDS, one, 0)

    pack_chunk(0, sig_ref, spread_ref, pack_ref)
    pl.semaphore_wait(barrier, SHARDS - 1 + 3)
    send_chunk(0)
    pack_chunk(1, sig_ref, spread_ref, pack_ref)
    send_chunk(1)

    make_decays(rates_ref, weights_ref, base_ref, gain_ref, leave_ref, hop_ref)
    block_states(sig_ref, base_ref, leave_ref, ends_ref, state_ref, left_ref)

    def to_row(source, target, sem):
        own = pltpu.make_async_copy(source.at[worker], target.at[worker], own_sem.at[sem])
        own.start()

        def one(step, _):
            to = lax.rem(worker + step, WORKERS)
            seq_copy(source.at[to], target.at[worker], send_sem.at[sem], recv_sem.at[sem], row * WORKERS + to).start()
            return _
        lax.fori_loop(1, WORKERS, one, 0)
        return own

    def settle_row(source, target, sem, own):
        own.wait()
        settle(source.at[pl.ds(0, WORKERS - 1)], send_sem.at[sem])
        settle(target.at[pl.ds(0, WORKERS - 1)], recv_sem.at[sem])

    own = to_row(left_ref, got_ref, 2)
    slide_ref[...] = jnp.zeros_like(slide_ref)
    settle_row(left_ref, got_ref, 2, own)

    tile_row = iota((TILES, LANES), 0)
    mode_rates = rates_ref[pl.ds(worker, 1), :]
    rate = jnp.where(
        lax.rem(tile_row, 2) == 0,
        jnp.broadcast_to(mode_rates[:, :LANES], (TILES, LANES)),
        jnp.broadcast_to(mode_rates[:, LANES:], (TILES, LANES)),
    )
    decay = jnp.exp(-float(ROWS) * rate)
    zero = jnp.zeros((TILES, LANES), F32)
    fore, back = owner_scan(decay, got_ref, (zero, zero), None)
    whole_ref[:TILES] = fore
    whole_ref[TILES:] = back
    for step in range(1, 4):
        to = lax.rem(row + step, 4)
        seq_copy(whole_ref, wholes_ref.at[row], send_sem.at[3], recv_sem.at[3], to * WORKERS + worker).start()
    wholes_ref[row] = whole_ref[...]
    for step in range(1, 4):
        settle(whole_ref, send_sem.at[3])
    settle(wholes_ref.at[pl.ds(0, 3)], recv_sem.at[3])
    fore, back = zero, zero
    for other in range(4):
        ahead = (row - 1 - other).astype(F32)
        behind = (other - 1 - row).astype(F32)
        length = float(ROWS * WORKERS)
        fore = fore + jnp.where(
            ahead >= 0.0, jnp.exp(-rate * (length * jnp.maximum(ahead, 0.0))), 0.0
        ) * wholes_ref[other, :TILES, :]
        back = back + jnp.where(
            behind >= 0.0, jnp.exp(-rate * (length * jnp.maximum(behind, 0.0))), 0.0
        ) * wholes_ref[other, TILES:, :]
    owner_scan(decay, got_ref, (fore, back), enter_ref)
    given_ref[...] = enter_ref[...].astype(BF16)
    own = to_row(given_ref, entered_ref, 4)

    def correlate_chunk(chunk):
        own_copies[chunk].wait()
        settle(pack_ref.at[chunk, pl.ds(0, (SHARDS - 1) * 16)], send_sem.at[chunk])
        settle(land_ref.at[chunk, pl.ds(0, (SHARDS - 1) * 16)], recv_sem.at[chunk])
        for half in range(2):
            rows_ref[half] = land_ref[chunk, :, half * LANES:(half + 1) * LANES].astype(F32)
        for low in range(2):
            share = correlate_filter(low, rows_ref, slide_ref, slid_ref, grad_ref, turn_ref, keep_ref, sums_ref)
            share_ref[2 * chunk + low] = share
            sent_ref[2 * chunk + low] = share.astype(BF16)

    correlate_chunk(0)

    settle_row(given_ref, entered_ref, 4, own)
    for mode in range(MODES):
        rows = entered_ref[mode].astype(F32)
        enter_ref[mode] = rows
    state_all = enter_ref[...].reshape(MODES * MODES, LANES)
    state_ref[...] = state_all
    for place in range(2 * TILES):
        first_ref[place] = state_ref[pl.ds(place, MODES, stride=2 * TILES), :]
    run_recurrence(sig_ref, base_ref, gain_ref, hop_ref, ends_ref, first_ref, long_ref)
    finish_outputs(q_ref, k_ref, v_ref, skip_ref, sig_ref, long_ref, layer_ref, kgrad_ref, vgrad_ref)

    correlate_chunk(1)

    for step in range(1, 4):
        to = lax.rem(chan + step, 4)
        pltpu.make_async_remote_copy(
            src_ref=sent_ref.at[to], dst_ref=came_ref.at[chan], send_sem=send_sem.at[5], recv_sem=recv_sem.at[5],
            device_id={"chan": to}, device_id_type=pl.DeviceIdType.MESH,
        ).start()
    settle(sent_ref.at[pl.ds(0, 3)], send_sem.at[5])
    settle(came_ref.at[pl.ds(0, 3)], recv_sem.at[5])
    came_ref[chan] = jnp.zeros((LANES, LANES), BF16)
    taps = share_ref[chan]
    for other in range(4):
        taps = taps + came_ref[other].astype(F32)
    for part in range(2):
        final_ref[:, part, :] = taps[part * SHARDS:(part + 1) * SHARDS]
    own = pltpu.make_async_copy(final_ref.at[seq], home_ref.at[seq], own_sem.at[5])
    own.start()

    def last(step, _):
        to = lax.rem(seq + step, SHARDS)
        seq_copy(final_ref.at[to], home_ref.at[seq], send_sem.at[6], recv_sem.at[6], to).start()
        return _
    lax.fori_loop(1, SHARDS, last, 0)
    own.wait()
    settle(final_ref.at[pl.ds(0, SHARDS - 1)], send_sem.at[6])
    settle(home_ref.at[pl.ds(0, SHARDS - 1)], recv_sem.at[6])
    scale = 1.0 / math.sqrt(SEQ_LEN * (CHANNELS // FILTERS))
    for part in range(2):
        taps_ref[:, part * LANES:(part + 1) * LANES] = home_ref[:, part, :] * scale


SCRATCH = [
    pltpu.VMEM((2, TILES, ROWS, LANES), F32),
    pltpu.VMEM((2, SHARDS * 16, LANES), F32),
    pltpu.VMEM((2, SHARDS * 16, ROWS), BF16),
    pltpu.VMEM((2, SHARDS * 16, ROWS), BF16),
    pltpu.VMEM((2, MODES, SUBS, LANES), F32),
    pltpu.VMEM((2, MODES, SUBS, LANES), F32),
    pltpu.VMEM((2, 2, MODES, SUBS, LANES), F32),
    pltpu.VMEM((2, 2, 3, MODES, SUBS, LANES), F32),
    pltpu.VMEM((2, TILES, MODES, SUBS, LANES), F32),
    pltpu.VMEM((2 * TILES * MODES, LANES), F32),
    pltpu.VMEM((WORKERS, 2 * TILES, LANES), BF16),
    pltpu.VMEM((WORKERS, 2 * TILES, LANES), BF16),
    pltpu.VMEM((2 * TILES, LANES), F32),
    pltpu.VMEM((4, 2 * TILES, LANES), F32),
    pltpu.VMEM((WORKERS, 2 * TILES, LANES), F32),
    pltpu.VMEM((WORKERS, 2 * TILES, LANES), BF16),
    pltpu.VMEM((WORKERS, 2 * TILES, LANES), BF16),
    pltpu.VMEM((2 * TILES, MODES, LANES), F32),
    pltpu.VMEM((2, TILES, ROWS, LANES), F32),
    pltpu.VMEM((2, SHARDS * 16, LANES), F32),
    pltpu.VMEM((4, 2, WINDOW, LANES), F32),
    pltpu.VMEM((4, 2 * ROWS, ROWS), BF16),
    pltpu.VMEM((2, ROWS, LANES), F32),
    pltpu.VMEM((ROWS, ROWS), BF16),
    pltpu.VMEM((2, LANES, LANES), F32),
    pltpu.VMEM((SHARDS * 2 * SUBS, LANES), F32),
    pltpu.VMEM((4, LANES, LANES), F32),
    pltpu.VMEM((4, LANES, LANES), BF16),
    pltpu.VMEM((4, LANES, LANES), BF16),
    pltpu.VMEM((SHARDS, 2, LANES), F32),
    pltpu.VMEM((SHARDS, 2, LANES), F32),
    pltpu.SemaphoreType.DMA((7,)),
    pltpu.SemaphoreType.DMA((7,)),
    pltpu.SemaphoreType.DMA((7,)),
]
VMEM = pl.BlockSpec(memory_space=pltpu.VMEM)


def per_device(query_proj, key_proj, value_proj, out_grad, residues, decay_rate, skip_gain):
    sds = jax.ShapeDtypeStruct
    layer, kgrad, vgrad, taps = pl.pallas_call(
        layer_kernel,
        out_shape=(sds((ROWS, 1024), BF16),) * 3 + (sds((SHARDS, ROWS), F32),),
        in_specs=[VMEM] * 7,
        out_specs=(VMEM,) * 4,
        scratch_shapes=SCRATCH,
        compiler_params=pltpu.CompilerParams(
            vmem_limit_bytes=56 * 2**20, collective_id=0, has_side_effects=True
        ),
    )(query_proj, key_proj, value_proj, out_grad, decay_rate.T, residues.T, skip_gain[None, :])
    return (layer, kgrad, vgrad, taps.T)


def solution(mesh):
    wide = P("seq", "chan")
    return jax.shard_map(
        per_device,
        mesh=mesh,
        in_specs=(wide, wide, wide, wide, P(), P(), P("chan")),
        out_specs=(wide, wide, wide, wide),
        check_vma=False,
    )
```

```python
import math

import jax
import jax.numpy as jnp
from jax import lax
from jax.experimental import pallas as pl
from jax.experimental.pallas import tpu as pltpu
from jax.sharding import PartitionSpec as P

CHANNELS = 4096
FILTERS = 256
MODES = 16
SEQ_LEN = 16384
SHARDS = 64
ROWS = 256
GROUPS = 4
F32 = jnp.float32
BF16 = jnp.bfloat16
LANES = 128
STEPS = 32
WORKERS = 16
SUBS = 8
TILES = 8
ACROSS = (((1,), (1,)), ((), ()))


def iota(shape, dim):
    return lax.broadcasted_iota(jnp.int32, shape, dim)


def identity(size):
    return (iota((size, size), 0) == iota((size, size), 1)).astype(BF16)


def reversal(size):
    row, col = iota((size, size), 0), iota((size, size), 1)
    return ((row + col == size) | ((row == 0) & (col == 0))).astype(BF16)


def load_signals(q_ref, k_ref, v_ref, o_ref, sig_ref):
    for tile in range(TILES):
        lanes = pl.ds(tile * LANES, LANES)
        conv_in = (k_ref[:, lanes].astype(F32) * v_ref[:, lanes].astype(F32)).astype(BF16)
        mid_grad = (o_ref[:, lanes].astype(F32) * q_ref[:, lanes].astype(F32)).astype(BF16)
        sig_ref[0, tile] = conv_in.astype(F32)
        sig_ref[1, tile] = mid_grad.astype(F32)


def pack_pair(pair, chan, sig_ref, spread_ref, pack_ref):
    eye = identity(LANES)
    rev = reversal(LANES)
    for group in range(GROUPS):
        tile = 2 * group + pair
        for sig in range(2):
            for half in range(2):
                block = sig_ref[sig, tile, half * LANES:(half + 1) * LANES, :].astype(BF16)
                if sig == 0:
                    block = jnp.dot(rev, block, preferred_element_type=F32).astype(BF16)
                turned = lax.dot_general(eye, block, ACROSS, preferred_element_type=F32)
                for low in range(2):
                    spread_ref[low, pl.ds(half * 8 + sig * 4 + group, SHARDS, stride=16), :] = turned[
                        low * SHARDS:(low + 1) * SHARDS
                    ]
    for low in range(2):
        pack_ref[lax.rem(2 * pair + low + 3 - chan, 4)] = spread_ref[low].astype(BF16)


def make_decays(rates_ref, weights_ref, base_ref, gain_ref, leave_ref, hop_ref):
    sub = iota((MODES, SUBS, LANES), 1)
    for side in range(2):
        lanes = slice(side * LANES, (side + 1) * LANES)
        rate = jnp.broadcast_to(rates_ref[:, lanes][:, None, :], (MODES, SUBS, LANES))
        weight = jnp.broadcast_to(weights_ref[:, lanes][:, None, :], (MODES, SUBS, LANES))
        base_ref[side] = jnp.exp(-rate)
        gain_ref[side] = weight * jnp.sqrt(rate)
        for sig in range(2):
            runs = SUBS - 1 - sub if sig == 0 else sub
            leave_ref[sig, side] = jnp.exp(-rate * (runs.astype(F32) * float(STEPS)))
            for at, hop in enumerate((1, 2, 4)):
                left = sub >= hop if sig == 0 else sub < SUBS - hop
                hop_ref[sig, side, at] = jnp.where(left, jnp.exp(-rate * float(STEPS * hop)), 0.0)


def block_states(sig_ref, base_ref, leave_ref, ends_ref, state_ref, state_out):
    def one_group(group, _):
        for side in range(2):
            tile = 2 * group + side
            base = base_ref[side]
            for sig in range(2):
                acc = None
                for step in range(STEPS):
                    place = step if sig == 0 else STEPS - 1 - step
                    row = sig_ref[sig, tile, pl.ds(place, SUBS, stride=STEPS), :]
                    wide = jnp.broadcast_to(row[None], (MODES, SUBS, LANES))
                    acc = wide if acc is None else base * acc + wide
                ends_ref[sig, tile] = acc
                start = pl.multiple_of((sig * TILES + tile) * MODES, MODES)
                state_ref[pl.ds(start, MODES), :] = jnp.sum(acc * leave_ref[sig, side], axis=1)
        return _
    lax.fori_loop(0, GROUPS, one_group, 0)
    for mode in range(MODES):
        state_out[mode] = state_ref[pl.ds(mode, 2 * TILES, stride=MODES), :].astype(BF16)


def owner_scan(decay, got_ref, first, enter_ref):
    fore, back = first
    for at in range(WORKERS):
        far = WORKERS - 1 - at
        if enter_ref is not None:
            enter_ref[at, :TILES, :] = fore
            enter_ref[far, TILES:, :] = back
        fore = decay * fore + got_ref[at, :, :].astype(F32)[:TILES]
        back = decay * back + got_ref[far, :, :].astype(F32)[TILES:]
    return fore, back


def run_recurrence(sig_ref, base_ref, gain_ref, hop_ref, ends_ref, enter_ref, long_ref):
    sub = iota((MODES, SUBS, LANES), 1)

    def one_group(group, _):
        for side in range(2):
            tile = 2 * group + side
            base, gain = base_ref[side], gain_ref[side]
            for sig in range(2):
                first = jnp.broadcast_to(enter_ref[sig * TILES + tile][:, None, :], (MODES, SUBS, LANES))
                ends = ends_ref[sig, tile]
                edge, turn = (0, 1) if sig == 0 else (SUBS - 1, SUBS - 1)
                held = jnp.where(sub == edge, first, pltpu.roll(ends, turn, 1))
                for at, hop in enumerate((1, 2, 4)):
                    moved = pltpu.roll(held, hop if sig == 0 else SUBS - hop, 1)
                    held = held + hop_ref[sig, side, at] * moved
                for step in range(STEPS):
                    place = step if sig == 0 else STEPS - 1 - step
                    where = pl.ds(place, SUBS, stride=STEPS)
                    row = sig_ref[sig, tile, where, :]
                    held = base * held + jnp.broadcast_to(row[None], (MODES, SUBS, LANES))
                    terms = gain * held
                    for width in (8, 4, 2, 1):
                        terms = terms[:width] + terms[width:]
                    long_ref[sig, tile, where, :] = terms[0]
        return _
    lax.fori_loop(0, GROUPS, one_group, 0)


def finish_outputs(q_ref, k_ref, v_ref, skip_ref, sig_ref, long_ref, layer_ref, kgrad_ref, vgrad_ref):
    for tile in range(TILES):
        lanes = pl.ds(tile * LANES, LANES)
        skip = skip_ref[:, lanes]
        layer = long_ref[0, tile] + skip * sig_ref[0, tile]
        layer_ref[:, lanes] = (q_ref[:, lanes].astype(F32) * layer).astype(BF16)
        total = long_ref[1, tile] + skip * sig_ref[1, tile]
        kgrad_ref[:, lanes] = (total * v_ref[:, lanes].astype(F32)).astype(BF16)
        vgrad_ref[:, lanes] = (total * k_ref[:, lanes].astype(F32)).astype(BF16)


PAD = ROWS


def correlate_filter(land_ref, rows_ref, slide_ref, slid_ref, grad_ref, turn_ref, sums_ref):
    rows_ref[...] = land_ref[...].astype(F32)
    for half in range(2):
        lanes = slice(half * LANES, (half + 1) * LANES)
        for group in range(GROUPS):
            conv_rows = rows_ref[pl.ds(half * 8 + group, SHARDS, stride=16), :]
            for early in range(4):
                slide_ref[early, half, pl.ds(group + 4 * early, SHARDS, stride=4), :] = conv_rows
            grad_ref[half, pl.ds(group, SHARDS, stride=4), :] = rows_ref[
                pl.ds(half * 8 + 4 + group, SHARDS, stride=16), :
            ]
        for early in range(4):
            slid_ref[early, PAD:, lanes] = slide_ref[early, half, :ROWS, :].astype(BF16)
        turn_ref[lanes, :] = lax.dot_general(
            identity(LANES), grad_ref[half].astype(BF16), ACROSS, preferred_element_type=F32
        ).astype(BF16)

    row, lane = iota((LANES, LANES), 0), iota((LANES, LANES), 1)
    causal = (lane == 0) | (row + lane >= LANES)

    def sheared(block):
        block = pltpu.roll(block, 0, 1, stride=1, stride_axis=0)
        return jnp.sum(block.reshape(LANES // SUBS, SUBS, LANES), axis=0)

    corner = later = jnp.zeros((LANES, LANES), F32)
    for block_lag in range(SHARDS - 1, -1, -1):
        start = PAD - 16 * (block_lag // 4)
        window = slid_ref[block_lag % 4, start:start + ROWS, :]
        prod = jnp.dot(turn_ref[...], window, preferred_element_type=F32)
        odd = prod[LANES:, :LANES] + corner
        even = prod[:LANES, :LANES] + prod[LANES:, LANES:]
        place = block_lag * 2 * SUBS
        sums_ref[place:place + SUBS, :] = sheared(jnp.where(causal, even, odd))
        sums_ref[place + SUBS:place + 2 * SUBS, :] = sheared(jnp.where(causal, odd, later))
        corner, later = prod[:LANES, LANES:], even

    out = []
    for part in range(2):
        total = sums_ref[pl.ds(part * SUBS, SHARDS, stride=2 * SUBS), :]
        for sub in range(1, SUBS):
            total = total + sums_ref[pl.ds(part * SUBS + sub, SHARDS, stride=2 * SUBS), :]
        out.append(total)
    return jnp.concatenate(out, axis=0)


def seq_copy(src, dst, send, recv, to):
    return pltpu.make_async_remote_copy(
        src_ref=src, dst_ref=dst, send_sem=send, recv_sem=recv,
        device_id={"seq": to}, device_id_type=pl.DeviceIdType.MESH,
    )


def settle(ref, sem):
    pltpu.make_async_copy(ref, ref, sem).wait()


STATES, TOTALS, ENTERING, SHARE, FINAL = 4, 5, 6, 7, 10


def layer_kernel(q_ref, k_ref, v_ref, o_ref, rates_ref, weights_ref, skip_ref,
                 layer_ref, kgrad_ref, vgrad_ref, taps_ref,
                 sig_ref, spread_ref, pack_ref, land_ref, base_ref, gain_ref, leave_ref, hop_ref, ends_ref,
                 state_ref, left_ref, got_ref, whole_ref, wholes_ref, enter_ref, given_ref, entered_ref, first_ref,
                 long_ref, rows_ref, slide_ref, slid_ref, grad_ref, turn_ref, sums_ref,
                 sent_ref, came_ref, final_ref, home_ref, send_sem, recv_sem, own_sem):
    seq, chan = lax.axis_index("seq"), lax.axis_index("chan")
    row, worker = lax.div(seq, WORKERS), lax.rem(seq, WORKERS)
    barrier = pltpu.get_barrier_semaphore()

    def greet(step, _):
        pl.semaphore_signal(barrier, inc=1, device_id={"seq": lax.rem(seq + step, SHARDS)}, device_id_type=pl.DeviceIdType.MESH)
        return _
    lax.fori_loop(1, SHARDS, greet, 0)
    for step in range(1, 4):
        pl.semaphore_signal(barrier, inc=1, device_id={"chan": lax.rem(chan + step, 4)}, device_id_type=pl.DeviceIdType.MESH)

    own_copies = {}

    def send_filter(place):
        mine = pl.ds(pl.multiple_of(seq * 16, 16), 16)
        own = pltpu.make_async_copy(pack_ref.at[place, mine], land_ref.at[place, mine], own_sem.at[place])
        own.start()
        own_copies[place] = own

        def one(step, _):
            to = lax.rem(seq + step, SHARDS)
            seq_copy(
                pack_ref.at[place, pl.ds(pl.multiple_of(to * 16, 16), 16)], land_ref.at[place, mine],
                send_sem.at[place], recv_sem.at[place], to,
            ).start()
            return _
        lax.fori_loop(1, SHARDS, one, 0)

    def to_row(source, target, sem):
        own = pltpu.make_async_copy(source.at[worker], target.at[worker], own_sem.at[sem])
        own.start()

        def one(step, _):
            to = lax.rem(worker + step, WORKERS)
            seq_copy(source.at[to], target.at[worker], send_sem.at[sem], recv_sem.at[sem], row * WORKERS + to).start()
            return _
        lax.fori_loop(1, WORKERS, one, 0)
        return own

    def settle_row(source, target, sem, own):
        own.wait()
        settle(source.at[pl.ds(0, WORKERS - 1)], send_sem.at[sem])
        settle(target.at[pl.ds(0, WORKERS - 1)], recv_sem.at[sem])

    def correlate(place):
        own_copies[place].wait()
        settle(pack_ref.at[place, pl.ds(0, (SHARDS - 1) * 16)], send_sem.at[place])
        settle(land_ref.at[place, pl.ds(0, (SHARDS - 1) * 16)], recv_sem.at[place])
        return correlate_filter(
            land_ref.at[place], rows_ref, slide_ref, slid_ref, grad_ref, turn_ref, sums_ref
        )

    def share_copy(place):
        return pltpu.make_async_remote_copy(
            src_ref=sent_ref.at[place], dst_ref=came_ref.at[place],
            send_sem=send_sem.at[SHARE + place], recv_sem=recv_sem.at[SHARE + place],
            device_id={"chan": lax.rem(chan + 1 + place, 4)}, device_id_type=pl.DeviceIdType.MESH,
        )

    def correlate_and_share(place):
        sent_ref[place] = correlate(place).astype(BF16)
        share_copy(place).start()

    load_signals(q_ref, k_ref, v_ref, o_ref, sig_ref)
    early_pair = lax.div(lax.rem(chan + 1, 4), 2)
    pack_pair(early_pair, chan, sig_ref, spread_ref, pack_ref)
    pl.semaphore_wait(barrier, SHARDS - 1 + 3)
    send_filter(0)

    make_decays(rates_ref, weights_ref, base_ref, gain_ref, leave_ref, hop_ref)
    block_states(sig_ref, base_ref, leave_ref, ends_ref, state_ref, left_ref)
    own_states = to_row(left_ref, got_ref, STATES)
    pack_pair(1 - early_pair, chan, sig_ref, spread_ref, pack_ref)
    send_filter(1)
    slide_ref[...] = jnp.zeros_like(slide_ref)
    slid_ref[:, :PAD, :] = jnp.zeros_like(slid_ref[:, :PAD, :])

    settle_row(left_ref, got_ref, STATES, own_states)
    tile_row = iota((TILES, LANES), 0)
    mode_rates = rates_ref[pl.ds(worker, 1), :]
    rate = jnp.where(
        lax.rem(tile_row, 2) == 0,
        jnp.broadcast_to(mode_rates[:, :LANES], (TILES, LANES)),
        jnp.broadcast_to(mode_rates[:, LANES:], (TILES, LANES)),
    )
    decay = jnp.exp(-float(ROWS) * rate)
    zero = jnp.zeros((TILES, LANES), F32)
    fore, back = owner_scan(decay, got_ref, (zero, zero), None)
    whole_ref[:TILES] = fore
    whole_ref[TILES:] = back
    for step in range(1, 4):
        to = lax.rem(row + step, 4)
        seq_copy(
            whole_ref, wholes_ref.at[row], send_sem.at[TOTALS], recv_sem.at[TOTALS], to * WORKERS + worker
        ).start()
    wholes_ref[row] = whole_ref[...]

    correlate_and_share(0)

    for step in range(1, 4):
        settle(whole_ref, send_sem.at[TOTALS])
    settle(wholes_ref.at[pl.ds(0, 3)], recv_sem.at[TOTALS])
    fore, back = zero, zero
    for other in range(4):
        ahead = (row - 1 - other).astype(F32)
        behind = (other - 1 - row).astype(F32)
        length = float(ROWS * WORKERS)
        fore = fore + jnp.where(
            ahead >= 0.0, jnp.exp(-rate * (length * jnp.maximum(ahead, 0.0))), 0.0
        ) * wholes_ref[other, :TILES, :]
        back = back + jnp.where(
            behind >= 0.0, jnp.exp(-rate * (length * jnp.maximum(behind, 0.0))), 0.0
        ) * wholes_ref[other, TILES:, :]
    owner_scan(decay, got_ref, (fore, back), enter_ref)
    given_ref[...] = enter_ref[...].astype(BF16)
    own_entering = to_row(given_ref, entered_ref, ENTERING)
    send_filter(2)

    correlate_and_share(1)
    send_filter(3)

    settle_row(given_ref, entered_ref, ENTERING, own_entering)
    state_ref[...] = entered_ref[...].astype(F32).reshape(MODES * MODES, LANES)
    for place in range(2 * TILES):
        first_ref[place] = state_ref[pl.ds(place, MODES, stride=2 * TILES), :]
    run_recurrence(sig_ref, base_ref, gain_ref, hop_ref, ends_ref, first_ref, long_ref)
    finish_outputs(q_ref, k_ref, v_ref, skip_ref, sig_ref, long_ref, layer_ref, kgrad_ref, vgrad_ref)

    correlate_and_share(2)
    taps = correlate(3)
    for place in range(3):
        share_copy(place).wait()
        taps = taps + came_ref[place].astype(F32)
    for part in range(2):
        final_ref[:, part, :] = taps[part * SHARDS:(part + 1) * SHARDS]
    own = pltpu.make_async_copy(final_ref.at[seq], home_ref.at[seq], own_sem.at[FINAL])
    own.start()

    def last(step, _):
        to = lax.rem(seq + step, SHARDS)
        seq_copy(final_ref.at[to], home_ref.at[seq], send_sem.at[FINAL], recv_sem.at[FINAL], to).start()
        return _
    lax.fori_loop(1, SHARDS, last, 0)
    own.wait()
    settle(final_ref.at[pl.ds(0, SHARDS - 1)], send_sem.at[FINAL])
    settle(home_ref.at[pl.ds(0, SHARDS - 1)], recv_sem.at[FINAL])
    scale = 1.0 / math.sqrt(SEQ_LEN * (CHANNELS // FILTERS))
    for part in range(2):
        taps_ref[:, part * LANES:(part + 1) * LANES] = home_ref[:, part, :] * scale


SCRATCH = [
    pltpu.VMEM((2, TILES, ROWS, LANES), F32),
    pltpu.VMEM((2, SHARDS * 16, LANES), F32),
    pltpu.VMEM((4, SHARDS * 16, LANES), BF16),
    pltpu.VMEM((4, SHARDS * 16, LANES), BF16),
    pltpu.VMEM((2, MODES, SUBS, LANES), F32),
    pltpu.VMEM((2, MODES, SUBS, LANES), F32),
    pltpu.VMEM((2, 2, MODES, SUBS, LANES), F32),
    pltpu.VMEM((2, 2, 3, MODES, SUBS, LANES), F32),
    pltpu.VMEM((2, TILES, MODES, SUBS, LANES), F32),
    pltpu.VMEM((2 * TILES * MODES, LANES), F32),
    pltpu.VMEM((WORKERS, 2 * TILES, LANES), BF16),
    pltpu.VMEM((WORKERS, 2 * TILES, LANES), BF16),
    pltpu.VMEM((2 * TILES, LANES), F32),
    pltpu.VMEM((4, 2 * TILES, LANES), F32),
    pltpu.VMEM((WORKERS, 2 * TILES, LANES), F32),
    pltpu.VMEM((WORKERS, 2 * TILES, LANES), BF16),
    pltpu.VMEM((WORKERS, 2 * TILES, LANES), BF16),
    pltpu.VMEM((2 * TILES, MODES, LANES), F32),
    pltpu.VMEM((2, TILES, ROWS, LANES), F32),
    pltpu.VMEM((SHARDS * 16, LANES), F32),
    pltpu.VMEM((4, 2, ROWS + 16, LANES), F32),
    pltpu.VMEM((4, 2 * ROWS, ROWS), BF16),
    pltpu.VMEM((2, ROWS, LANES), F32),
    pltpu.VMEM((ROWS, ROWS), BF16),
    pltpu.VMEM((SHARDS * 2 * SUBS, LANES), F32),
    pltpu.VMEM((3, LANES, LANES), BF16),
    pltpu.VMEM((3, LANES, LANES), BF16),
    pltpu.VMEM((SHARDS, 2, LANES), F32),
    pltpu.VMEM((SHARDS, 2, LANES), F32),
    pltpu.SemaphoreType.DMA((11,)),
    pltpu.SemaphoreType.DMA((11,)),
    pltpu.SemaphoreType.DMA((11,)),
]
VMEM = pl.BlockSpec(memory_space=pltpu.VMEM)


def per_device(query_proj, key_proj, value_proj, out_grad, residues, decay_rate, skip_gain):
    sds = jax.ShapeDtypeStruct
    layer, kgrad, vgrad, taps = pl.pallas_call(
        layer_kernel,
        out_shape=(sds((ROWS, 1024), BF16),) * 3 + (sds((SHARDS, ROWS), F32),),
        in_specs=[VMEM] * 7,
        out_specs=(VMEM,) * 4,
        scratch_shapes=SCRATCH,
        compiler_params=pltpu.CompilerParams(
            vmem_limit_bytes=56 * 2**20, collective_id=0, has_side_effects=True
        ),
    )(query_proj, key_proj, value_proj, out_grad, decay_rate.T, residues.T, skip_gain[None, :])
    return (layer, kgrad, vgrad, taps.T)


def solution(mesh):
    wide = P("seq", "chan")
    return jax.shard_map(
        per_device,
        mesh=mesh,
        in_specs=(wide, wide, wide, wide, P(), P(), P("chan")),
        out_specs=(wide, wide, wide, wide),
        check_vma=False,
    )
```

```python
import math

import jax
import jax.numpy as jnp
from jax import lax
from jax.experimental import pallas as pl
from jax.experimental.pallas import tpu as pltpu
from jax.sharding import PartitionSpec as P

CHANNELS = 4096
FILTERS = 256
MODES = 16
SEQ_LEN = 16384
SHARDS = 64
ROWS = 256
GROUPS = 4
F32 = jnp.float32
BF16 = jnp.bfloat16
LANES = 128
STEPS = 32
WORKERS = 16
SUBS = 8
TILES = 8
ACROSS = (((1,), (1,)), ((), ()))


def iota(shape, dim):
    return lax.broadcasted_iota(jnp.int32, shape, dim)


def identity(size):
    return (iota((size, size), 0) == iota((size, size), 1)).astype(BF16)


def reversal(size):
    row, col = iota((size, size), 0), iota((size, size), 1)
    return ((row + col == size) | ((row == 0) & (col == 0))).astype(BF16)


def load_signals(tile, in_ref, sig_ref):
    query, key, value, grad = (in_ref[at, tile].astype(F32) for at in range(4))
    sig_ref[0, tile] = (key * value).astype(BF16).astype(F32)
    sig_ref[1, tile] = (grad * query).astype(BF16).astype(F32)


def pack_pair(pair, chan, sig_ref, spread_ref, pack_ref):
    eye = identity(LANES)
    rev = reversal(LANES)
    for group in range(GROUPS):
        tile = 2 * group + pair
        for sig in range(2):
            for half in range(2):
                block = sig_ref[sig, tile, half * LANES:(half + 1) * LANES, :].astype(BF16)
                if sig == 0:
                    block = jnp.dot(rev, block, preferred_element_type=F32).astype(BF16)
                turned = lax.dot_general(eye, block, ACROSS, preferred_element_type=F32)
                for low in range(2):
                    spread_ref[low, pl.ds(half * 8 + sig * 4 + group, SHARDS, stride=16), :] = turned[
                        low * SHARDS:(low + 1) * SHARDS
                    ]
    for low in range(2):
        pack_ref[lax.rem(2 * pair + low + 3 - chan, 4)] = spread_ref[low].astype(BF16)


def make_decays(rates_ref, weights_ref, base_ref, gain_ref, leave_ref, hop_ref):
    sub = iota((MODES, SUBS, LANES), 1)
    for side in range(2):
        rows = slice(side * MODES, (side + 1) * MODES)
        rate = jnp.broadcast_to(rates_ref[rows, :][:, None, :], (MODES, SUBS, LANES))
        weight = jnp.broadcast_to(weights_ref[rows, :][:, None, :], (MODES, SUBS, LANES))
        base_ref[side] = jnp.exp(-rate)
        gain_ref[side] = weight * jnp.sqrt(rate)
        for sig in range(2):
            runs = SUBS - 1 - sub if sig == 0 else sub
            leave_ref[sig, side] = jnp.exp(-rate * (runs.astype(F32) * float(STEPS)))
            for at, hop in enumerate((1, 2, 4)):
                left = sub >= hop if sig == 0 else sub < SUBS - hop
                hop_ref[sig, side, at] = jnp.where(left, jnp.exp(-rate * float(STEPS * hop)), 0.0)


def block_states(sig_ref, base_ref, leave_ref, ends_ref, state_ref, state_out):
    def one_group(group, _):
        for side in range(2):
            tile = 2 * group + side
            base = base_ref[side]
            for sig in range(2):
                acc = None
                for step in range(STEPS):
                    place = step if sig == 0 else STEPS - 1 - step
                    row = sig_ref[sig, tile, pl.ds(place, SUBS, stride=STEPS), :]
                    wide = jnp.broadcast_to(row[None], (MODES, SUBS, LANES))
                    acc = wide if acc is None else base * acc + wide
                ends_ref[sig, tile] = acc
                start = pl.multiple_of((sig * TILES + tile) * MODES, MODES)
                state_ref[pl.ds(start, MODES), :] = jnp.sum(acc * leave_ref[sig, side], axis=1)
        return _
    lax.fori_loop(0, GROUPS, one_group, 0)
    for mode in range(MODES):
        state_out[mode] = state_ref[pl.ds(mode, 2 * TILES, stride=MODES), :].astype(BF16)


def owner_scan(decay, got_ref, first, enter_ref):
    fore, back = first
    for at in range(WORKERS):
        far = WORKERS - 1 - at
        if enter_ref is not None:
            enter_ref[at, :TILES, :] = fore
            enter_ref[far, TILES:, :] = back
        fore = decay * fore + got_ref[at, :, :].astype(F32)[:TILES]
        back = decay * back + got_ref[far, :, :].astype(F32)[TILES:]
    return fore, back


def run_recurrence(sig_ref, base_ref, gain_ref, hop_ref, ends_ref, enter_ref, long_ref):
    sub = iota((MODES, SUBS, LANES), 1)

    def one_group(group, _):
        for side in range(2):
            tile = 2 * group + side
            base, gain = base_ref[side], gain_ref[side]
            for sig in range(2):
                first = jnp.broadcast_to(enter_ref[sig * TILES + tile][:, None, :], (MODES, SUBS, LANES))
                ends = ends_ref[sig, tile]
                edge, turn = (0, 1) if sig == 0 else (SUBS - 1, SUBS - 1)
                held = jnp.where(sub == edge, first, pltpu.roll(ends, turn, 1))
                for at, hop in enumerate((1, 2, 4)):
                    moved = pltpu.roll(held, hop if sig == 0 else SUBS - hop, 1)
                    held = held + hop_ref[sig, side, at] * moved
                for step in range(STEPS):
                    place = step if sig == 0 else STEPS - 1 - step
                    where = pl.ds(place, SUBS, stride=STEPS)
                    row = sig_ref[sig, tile, where, :]
                    held = base * held + jnp.broadcast_to(row[None], (MODES, SUBS, LANES))
                    terms = gain * held
                    for width in (8, 4, 2, 1):
                        terms = terms[:width] + terms[width:]
                    long_ref[sig, tile, where, :] = terms[0]
        return _
    lax.fori_loop(0, GROUPS, one_group, 0)


def finish_outputs(in_ref, skip_ref, sig_ref, long_ref, layer_ref, kgrad_ref, vgrad_ref):
    for tile in range(TILES):
        lanes = pl.ds(tile * LANES, LANES)
        skip = skip_ref[tile:tile + 1, :]
        layer = long_ref[0, tile] + skip * sig_ref[0, tile]
        layer_ref[:, lanes] = (in_ref[0, tile].astype(F32) * layer).astype(BF16)
        total = long_ref[1, tile] + skip * sig_ref[1, tile]
        kgrad_ref[:, lanes] = (total * in_ref[2, tile].astype(F32)).astype(BF16)
        vgrad_ref[:, lanes] = (total * in_ref[1, tile].astype(F32)).astype(BF16)


PAD = ROWS
HALF = SHARDS // 2


def prepare_filter(land_ref, rows_ref, slide_ref, slid_ref, grad_ref, turn_ref):
    rows_ref[...] = land_ref[...].astype(F32)
    for half in range(2):
        lanes = slice(half * LANES, (half + 1) * LANES)
        for group in range(GROUPS):
            conv_rows = rows_ref[pl.ds(half * 8 + group, SHARDS, stride=16), :]
            for early in range(4):
                slide_ref[early, half, pl.ds(group + 4 * early, SHARDS, stride=4), :] = conv_rows
            grad_ref[half, pl.ds(group, SHARDS, stride=4), :] = rows_ref[
                pl.ds(half * 8 + 4 + group, SHARDS, stride=16), :
            ]
        for early in range(4):
            slid_ref[early, PAD:, lanes] = slide_ref[early, half, :ROWS, :].astype(BF16)
        turn_ref[lanes, :] = lax.dot_general(
            identity(LANES), grad_ref[half].astype(BF16), ACROSS, preferred_element_type=F32
        ).astype(BF16)


def lag_product(block_lag, slid_ref, turn_ref):
    start = PAD - 16 * (block_lag // 4)
    if not isinstance(start, int):
        start = pl.multiple_of(start, 16)
    window = slid_ref[block_lag % 4, pl.ds(start, ROWS), :]
    return jnp.dot(turn_ref[...], window, preferred_element_type=F32)


def lag_rows(prod, corner, later):
    row, lane = iota((LANES, LANES), 0), iota((LANES, LANES), 1)
    causal = (lane == 0) | (row + lane >= LANES)

    def sheared(block):
        block = pltpu.roll(block, 0, 1, stride=1, stride_axis=0)
        return jnp.sum(block.reshape(LANES // SUBS, SUBS, LANES), axis=0)

    odd = prod[LANES:, :LANES] + corner
    even = prod[:LANES, :LANES] + prod[LANES:, LANES:]
    pair = (sheared(jnp.where(causal, even, odd)), sheared(jnp.where(causal, odd, later)))
    return pair, prod[:LANES, LANES:], even


def correlate_lags(longest, shortest, carried, slid_ref, turn_ref, sums_ref):
    corner, later = carried
    for block_lag in range(longest, shortest - 1, -1):
        pair, corner, later = lag_rows(lag_product(block_lag, slid_ref, turn_ref), corner, later)
        place = block_lag * 2 * SUBS
        sums_ref[place:place + SUBS, :] = pair[0]
        sums_ref[place + SUBS:place + 2 * SUBS, :] = pair[1]

    out = []
    count = longest - shortest + 1
    for part in range(2):
        total = None
        for sub in range(SUBS):
            start = (shortest * 2 + part) * SUBS + sub
            rows = sums_ref[pl.ds(start, count, stride=2 * SUBS), :]
            total = rows if total is None else total + rows
        out.append(total)
    return out, (corner, later)


def no_carry():
    return (jnp.zeros((LANES, LANES), F32),) * 2


def seq_copy(src, dst, send, recv, to):
    return pltpu.make_async_remote_copy(
        src_ref=src, dst_ref=dst, send_sem=send, recv_sem=recv,
        device_id={"seq": to}, device_id_type=pl.DeviceIdType.MESH,
    )


def settle(ref, sem):
    pltpu.make_async_copy(ref, ref, sem).wait()


STATES, TOTALS, ENTERING, SHARE, FINAL = 4, 5, 6, 7, 10


def layer_kernel(q_ref, k_ref, v_ref, o_ref, small_ref,
                 layer_ref, kgrad_ref, vgrad_ref, taps_ref,
                 in_ref, sig_ref, spread_ref, pack_ref, land_ref, base_ref, gain_ref, leave_ref, hop_ref, ends_ref,
                 state_ref, left_ref, got_ref, whole_ref, wholes_ref, enter_ref, given_ref, entered_ref, first_ref,
                 long_ref, rows_ref, slide_ref, slid_ref, grad_ref, turn_ref, sums_ref,
                 sent_ref, came_ref, final_ref, home_ref, send_sem, recv_sem, own_sem, in_sem):
    seq, chan = lax.axis_index("seq"), lax.axis_index("chan")
    row, worker = lax.div(seq, WORKERS), lax.rem(seq, WORKERS)
    rates_ref, weights_ref = small_ref.at[:2 * MODES], small_ref.at[2 * MODES:4 * MODES]
    skip_ref = small_ref.at[4 * MODES:]
    early_pair = lax.div(lax.rem(chan + 1, 4), 2)
    pairs = (early_pair, 1 - early_pair)

    for wave, pair in enumerate(pairs):
        for group in range(GROUPS):
            tile = 2 * group + pair
            for at, source in enumerate((q_ref, k_ref, v_ref, o_ref)):
                pltpu.make_async_copy(
                    source.at[:, pl.ds(pl.multiple_of(tile * LANES, LANES), LANES)],
                    in_ref.at[at, tile], in_sem.at[wave],
                ).start()

    def load_pair(wave):
        settle(in_ref.at[pl.ds(0, 2)], in_sem.at[wave])
        for group in range(GROUPS):
            load_signals(2 * group + pairs[wave], in_ref, sig_ref)

    barrier = pltpu.get_barrier_semaphore()

    def greet(step, _):
        pl.semaphore_signal(barrier, inc=1, device_id={"seq": lax.rem(seq + step, SHARDS)}, device_id_type=pl.DeviceIdType.MESH)
        return _
    lax.fori_loop(1, SHARDS, greet, 0)
    for step in range(1, 4):
        pl.semaphore_signal(barrier, inc=1, device_id={"chan": lax.rem(chan + step, 4)}, device_id_type=pl.DeviceIdType.MESH)

    own_copies = {}

    def send_filter(place):
        mine = pl.ds(pl.multiple_of(seq * 16, 16), 16)
        own = pltpu.make_async_copy(pack_ref.at[place, mine], land_ref.at[place, mine], own_sem.at[place])
        own.start()
        own_copies[place] = own

        def one(step, _):
            to = lax.rem(seq + step, SHARDS)
            seq_copy(
                pack_ref.at[place, pl.ds(pl.multiple_of(to * 16, 16), 16)], land_ref.at[place, mine],
                send_sem.at[place], recv_sem.at[place], to,
            ).start()
            return _
        lax.fori_loop(1, SHARDS, one, 0)

    def to_row(source, target, sem):
        own = pltpu.make_async_copy(source.at[worker], target.at[worker], own_sem.at[sem])
        own.start()

        def one(step, _):
            to = lax.rem(worker + step, WORKERS)
            seq_copy(source.at[to], target.at[worker], send_sem.at[sem], recv_sem.at[sem], row * WORKERS + to).start()
            return _
        lax.fori_loop(1, WORKERS, one, 0)
        return own

    def settle_row(source, target, sem, own):
        own.wait()
        settle(source.at[pl.ds(0, WORKERS - 1)], send_sem.at[sem])
        settle(target.at[pl.ds(0, WORKERS - 1)], recv_sem.at[sem])

    def prepare(place):
        own_copies[place].wait()
        settle(pack_ref.at[place, pl.ds(0, (SHARDS - 1) * 16)], send_sem.at[place])
        settle(land_ref.at[place, pl.ds(0, (SHARDS - 1) * 16)], recv_sem.at[place])
        prepare_filter(land_ref.at[place], rows_ref, slide_ref, slid_ref, grad_ref, turn_ref)

    def share_copy(place):
        return pltpu.make_async_remote_copy(
            src_ref=sent_ref.at[place], dst_ref=came_ref.at[place],
            send_sem=send_sem.at[SHARE + place], recv_sem=recv_sem.at[SHARE + place],
            device_id={"chan": lax.rem(chan + 1 + place, 4)}, device_id_type=pl.DeviceIdType.MESH,
        )

    def correlate_and_share(place):
        prepare(place)
        parts, _ = correlate_lags(SHARDS - 1, 0, no_carry(), slid_ref, turn_ref, sums_ref)
        sent_ref[place] = jnp.concatenate(parts, axis=0).astype(BF16)
        share_copy(place).start()

    make_decays(rates_ref, weights_ref, base_ref, gain_ref, leave_ref, hop_ref)
    slide_ref[...] = jnp.zeros_like(slide_ref)
    slid_ref[:, :PAD, :] = jnp.zeros_like(slid_ref[:, :PAD, :])

    load_pair(0)
    pack_pair(early_pair, chan, sig_ref, spread_ref, pack_ref)
    pl.semaphore_wait(barrier, SHARDS - 1 + 3)
    send_filter(0)

    load_pair(1)
    block_states(sig_ref, base_ref, leave_ref, ends_ref, state_ref, left_ref)
    own_states = to_row(left_ref, got_ref, STATES)
    pack_pair(1 - early_pair, chan, sig_ref, spread_ref, pack_ref)
    send_filter(1)

    settle_row(left_ref, got_ref, STATES, own_states)
    tile_row = iota((TILES, LANES), 0)
    rate = jnp.where(
        lax.rem(tile_row, 2) == 0,
        jnp.broadcast_to(rates_ref[pl.ds(worker, 1), :], (TILES, LANES)),
        jnp.broadcast_to(rates_ref[pl.ds(MODES + worker, 1), :], (TILES, LANES)),
    )
    decay = jnp.exp(-float(ROWS) * rate)
    zero = jnp.zeros((TILES, LANES), F32)
    fore, back = owner_scan(decay, got_ref, (zero, zero), None)
    whole_ref[:TILES] = fore
    whole_ref[TILES:] = back
    for step in range(1, 4):
        to = lax.rem(row + step, 4)
        seq_copy(
            whole_ref, wholes_ref.at[row], send_sem.at[TOTALS], recv_sem.at[TOTALS], to * WORKERS + worker
        ).start()
    wholes_ref[row] = whole_ref[...]

    correlate_and_share(0)

    for step in range(1, 4):
        settle(whole_ref, send_sem.at[TOTALS])
    settle(wholes_ref.at[pl.ds(0, 3)], recv_sem.at[TOTALS])
    fore, back = zero, zero
    for other in range(4):
        ahead = (row - 1 - other).astype(F32)
        behind = (other - 1 - row).astype(F32)
        length = float(ROWS * WORKERS)
        fore = fore + jnp.where(
            ahead >= 0.0, jnp.exp(-rate * (length * jnp.maximum(ahead, 0.0))), 0.0
        ) * wholes_ref[other, :TILES, :]
        back = back + jnp.where(
            behind >= 0.0, jnp.exp(-rate * (length * jnp.maximum(behind, 0.0))), 0.0
        ) * wholes_ref[other, TILES:, :]
    owner_scan(decay, got_ref, (fore, back), enter_ref)
    given_ref[...] = enter_ref[...].astype(BF16)
    own_entering = to_row(given_ref, entered_ref, ENTERING)
    send_filter(2)

    correlate_and_share(1)
    send_filter(3)

    settle_row(given_ref, entered_ref, ENTERING, own_entering)
    state_ref[...] = entered_ref[...].astype(F32).reshape(MODES * MODES, LANES)
    for place in range(2 * TILES):
        first_ref[place] = state_ref[pl.ds(place, MODES, stride=2 * TILES), :]
    run_recurrence(sig_ref, base_ref, gain_ref, hop_ref, ends_ref, first_ref, long_ref)
    finish_outputs(in_ref, skip_ref, sig_ref, long_ref, layer_ref, kgrad_ref, vgrad_ref)

    correlate_and_share(2)
    prepare(3)
    carried = no_carry()
    for upper in (1, 0):
        low = upper * HALF
        parts, carried = correlate_lags(low + HALF - 1, low, carried, slid_ref, turn_ref, sums_ref)
        if upper:
            for place in range(3):
                share_copy(place).wait()
        for part in range(2):
            rows = slice(part * SHARDS + low, part * SHARDS + low + HALF)
            shares = came_ref[0, rows, :].astype(F32) + came_ref[1, rows, :].astype(F32) + came_ref[2, rows, :].astype(F32)
            final_ref[low:low + HALF, part, :] = parts[part] + shares

        def leave(step, _):
            to = low + lax.rem(seq + step, HALF)

            @pl.when(to != seq)
            def _send():
                seq_copy(final_ref.at[to], home_ref.at[seq], send_sem.at[FINAL], recv_sem.at[FINAL], to).start()
            return _
        lax.fori_loop(0, HALF, leave, 0)
    home_ref[seq] = final_ref[seq]
    settle(final_ref.at[pl.ds(0, SHARDS - 1)], send_sem.at[FINAL])
    settle(home_ref.at[pl.ds(0, SHARDS - 1)], recv_sem.at[FINAL])
    scale = 1.0 / math.sqrt(SEQ_LEN * (CHANNELS // FILTERS))
    for part in range(2):
        taps_ref[:, part * LANES:(part + 1) * LANES] = home_ref[:, part, :] * scale


def hand_on(*refs):
    sources, targets, sem = refs[:4], refs[4:8], refs[8]
    pieces = []
    for at, source in enumerate(sources):
        count = 4 if at < 3 else 1
        rows = source.shape[0] // count
        for piece in range(count):
            some = pl.ds(piece * rows, rows)
            pieces.append(pltpu.make_async_copy(source.at[some], targets[at].at[some], sem.at[at * 4 + piece]))
    for copy in pieces:
        copy.start()
    for copy in pieces:
        copy.wait()


SCRATCH = [
    pltpu.VMEM((4, TILES, ROWS, LANES), BF16),
    pltpu.VMEM((2, TILES, ROWS, LANES), F32),
    pltpu.VMEM((2, SHARDS * 16, LANES), F32),
    pltpu.VMEM((4, SHARDS * 16, LANES), BF16),
    pltpu.VMEM((4, SHARDS * 16, LANES), BF16),
    pltpu.VMEM((2, MODES, SUBS, LANES), F32),
    pltpu.VMEM((2, MODES, SUBS, LANES), F32),
    pltpu.VMEM((2, 2, MODES, SUBS, LANES), F32),
    pltpu.VMEM((2, 2, 3, MODES, SUBS, LANES), F32),
    pltpu.VMEM((2, TILES, MODES, SUBS, LANES), F32),
    pltpu.VMEM((2 * TILES * MODES, LANES), F32),
    pltpu.VMEM((WORKERS, 2 * TILES, LANES), BF16),
    pltpu.VMEM((WORKERS, 2 * TILES, LANES), BF16),
    pltpu.VMEM((2 * TILES, LANES), F32),
    pltpu.VMEM((4, 2 * TILES, LANES), F32),
    pltpu.VMEM((WORKERS, 2 * TILES, LANES), F32),
    pltpu.VMEM((WORKERS, 2 * TILES, LANES), BF16),
    pltpu.VMEM((WORKERS, 2 * TILES, LANES), BF16),
    pltpu.VMEM((2 * TILES, MODES, LANES), F32),
    pltpu.VMEM((2, TILES, ROWS, LANES), F32),
    pltpu.VMEM((SHARDS * 16, LANES), F32),
    pltpu.VMEM((4, 2, ROWS + 16, LANES), F32),
    pltpu.VMEM((4, 2 * ROWS, ROWS), BF16),
    pltpu.VMEM((2, ROWS, LANES), F32),
    pltpu.VMEM((ROWS, ROWS), BF16),
    pltpu.VMEM((SHARDS * 2 * SUBS, LANES), F32),
    pltpu.VMEM((3, LANES, LANES), BF16),
    pltpu.VMEM((3, LANES, LANES), BF16),
    pltpu.VMEM((SHARDS, 2, LANES), F32),
    pltpu.VMEM((SHARDS, 2, LANES), F32),
    pltpu.SemaphoreType.DMA((11,)),
    pltpu.SemaphoreType.DMA((11,)),
    pltpu.SemaphoreType.DMA((11,)),
    pltpu.SemaphoreType.DMA((2,)),
]
VMEM = pl.BlockSpec(memory_space=pltpu.VMEM)


ANY = pl.BlockSpec(memory_space=pl.ANY)


def per_device(query_proj, key_proj, value_proj, out_grad, residues, decay_rate, skip_gain):
    sds = jax.ShapeDtypeStruct
    shapes = (sds((ROWS, 1024), BF16),) * 3 + (sds((SHARDS, ROWS), F32),)
    sides = [table.T[:, side * LANES:(side + 1) * LANES] for table in (decay_rate, residues) for side in range(2)]
    small = jnp.concatenate(sides + [skip_gain.reshape(TILES, LANES)], axis=0)
    results = pl.pallas_call(
        layer_kernel,
        out_shape=shapes,
        in_specs=[ANY] * 4 + [VMEM],
        out_specs=(VMEM,) * 4,
        scratch_shapes=SCRATCH,
        compiler_params=pltpu.CompilerParams(
            vmem_limit_bytes=53120 * 2**10, collective_id=0, has_side_effects=True
        ),
    )(query_proj, key_proj, value_proj, out_grad, small)
    layer, kgrad, vgrad, taps = pl.pallas_call(
        hand_on,
        out_shape=shapes,
        in_specs=[pl.BlockSpec(memory_space=pltpu.VMEM)] * 4,
        out_specs=(pl.BlockSpec(memory_space=pltpu.HBM),) * 4,
        scratch_shapes=[pltpu.SemaphoreType.DMA((16,))],
        compiler_params=pltpu.CompilerParams(vmem_limit_bytes=53120 * 2**10),
    )(*results)
    return (layer, kgrad, vgrad, taps.T)


def solution(mesh):
    wide = P("seq", "chan")
    return jax.shard_map(
        per_device,
        mesh=mesh,
        in_specs=(wide, wide, wide, wide, P(), P(), P("chan")),
        out_specs=(wide, wide, wide, wide),
        check_vma=False,
    )
```

```python
import math

import jax
import jax.numpy as jnp
from jax import lax
from jax.experimental import pallas as pl
from jax.experimental.pallas import tpu as pltpu
from jax.sharding import PartitionSpec as P

CHANNELS = 4096
FILTERS = 256
MODES = 16
SEQ_LEN = 16384
SHARDS = 64
ROWS = 256
GROUPS = 4
F32 = jnp.float32
BF16 = jnp.bfloat16
LANES = 128
STEPS = 32
WORKERS = 16
SUBS = 8
TILES = 8
ACROSS = (((1,), (1,)), ((), ()))


def iota(shape, dim):
    return lax.broadcasted_iota(jnp.int32, shape, dim)


def identity(size):
    return (iota((size, size), 0) == iota((size, size), 1)).astype(BF16)


def reversal(size):
    row, col = iota((size, size), 0), iota((size, size), 1)
    return ((row + col == size) | ((row == 0) & (col == 0))).astype(BF16)


def load_signals(tile, in_ref, sig_ref):
    query, key, value, grad = (in_ref[at, tile].astype(F32) for at in range(4))
    sig_ref[0, tile] = (key * value).astype(BF16).astype(F32)
    sig_ref[1, tile] = (grad * query).astype(BF16).astype(F32)


def pack_pair(pair, chan, sig_ref, spread_ref, pack_ref):
    eye = identity(LANES)
    rev = reversal(LANES)
    for group in range(GROUPS):
        tile = 2 * group + pair
        for sig in range(2):
            for half in range(2):
                block = sig_ref[sig, tile, half * LANES:(half + 1) * LANES, :].astype(BF16)
                if sig == 0:
                    block = jnp.dot(rev, block, preferred_element_type=F32).astype(BF16)
                turned = lax.dot_general(eye, block, ACROSS, preferred_element_type=F32)
                for low in range(2):
                    spread_ref[low, pl.ds(half * 8 + sig * 4 + group, SHARDS, stride=16), :] = turned[
                        low * SHARDS:(low + 1) * SHARDS
                    ]
    for low in range(2):
        pack_ref[lax.rem(2 * pair + low + 3 - chan, 4)] = spread_ref[low].astype(BF16)


def make_decays(rates_ref, weights_ref, base_ref, gain_ref, leave_ref, hop_ref):
    sub = iota((MODES, SUBS, LANES), 1)
    for side in range(2):
        lanes = slice(side * LANES, (side + 1) * LANES)
        rate = jnp.broadcast_to(rates_ref[:, lanes][:, None, :], (MODES, SUBS, LANES))
        weight = jnp.broadcast_to(weights_ref[:, lanes][:, None, :], (MODES, SUBS, LANES))
        base_ref[side] = jnp.exp(-rate)
        gain_ref[side] = weight * jnp.sqrt(rate)
        for sig in range(2):
            runs = SUBS - 1 - sub if sig == 0 else sub
            leave_ref[sig, side] = jnp.exp(-rate * (runs.astype(F32) * float(STEPS)))
            for at, hop in enumerate((1, 2, 4)):
                left = sub >= hop if sig == 0 else sub < SUBS - hop
                hop_ref[sig, side, at] = jnp.where(left, jnp.exp(-rate * float(STEPS * hop)), 0.0)


def block_states(sig_ref, base_ref, leave_ref, ends_ref, state_ref, state_out):
    def one_group(group, _):
        for side in range(2):
            tile = 2 * group + side
            base = base_ref[side]
            for sig in range(2):
                acc = None
                for step in range(STEPS):
                    place = step if sig == 0 else STEPS - 1 - step
                    row = sig_ref[sig, tile, pl.ds(place, SUBS, stride=STEPS), :]
                    wide = jnp.broadcast_to(row[None], (MODES, SUBS, LANES))
                    acc = wide if acc is None else base * acc + wide
                ends_ref[sig, tile] = acc
                start = pl.multiple_of((sig * TILES + tile) * MODES, MODES)
                state_ref[pl.ds(start, MODES), :] = jnp.sum(acc * leave_ref[sig, side], axis=1)
        return _
    lax.fori_loop(0, GROUPS, one_group, 0)
    for mode in range(MODES):
        state_out[mode] = state_ref[pl.ds(mode, 2 * TILES, stride=MODES), :].astype(BF16)


def owner_scan(decay, got_ref, first, enter_ref):
    fore, back = first
    for at in range(WORKERS):
        far = WORKERS - 1 - at
        if enter_ref is not None:
            enter_ref[at, :TILES, :] = fore
            enter_ref[far, TILES:, :] = back
        fore = decay * fore + got_ref[at, :, :].astype(F32)[:TILES]
        back = decay * back + got_ref[far, :, :].astype(F32)[TILES:]
    return fore, back


def run_recurrence(sig_ref, base_ref, gain_ref, hop_ref, ends_ref, enter_ref, long_ref):
    sub = iota((MODES, SUBS, LANES), 1)

    def one_group(group, _):
        for side in range(2):
            tile = 2 * group + side
            base, gain = base_ref[side], gain_ref[side]
            for sig in range(2):
                first = jnp.broadcast_to(enter_ref[sig * TILES + tile][:, None, :], (MODES, SUBS, LANES))
                ends = ends_ref[sig, tile]
                edge, turn = (0, 1) if sig == 0 else (SUBS - 1, SUBS - 1)
                held = jnp.where(sub == edge, first, pltpu.roll(ends, turn, 1))
                for at, hop in enumerate((1, 2, 4)):
                    moved = pltpu.roll(held, hop if sig == 0 else SUBS - hop, 1)
                    held = held + hop_ref[sig, side, at] * moved
                for step in range(STEPS):
                    place = step if sig == 0 else STEPS - 1 - step
                    where = pl.ds(place, SUBS, stride=STEPS)
                    row = sig_ref[sig, tile, where, :]
                    held = base * held + jnp.broadcast_to(row[None], (MODES, SUBS, LANES))
                    terms = gain * held
                    for width in (8, 4, 2, 1):
                        terms = terms[:width] + terms[width:]
                    long_ref[sig, tile, where, :] = terms[0]
        return _
    lax.fori_loop(0, GROUPS, one_group, 0)


def finish_outputs(in_ref, skip_ref, sig_ref, long_ref, layer_ref, kgrad_ref, vgrad_ref):
    for tile in range(TILES):
        lanes = pl.ds(tile * LANES, LANES)
        skip = skip_ref[tile // 2:tile // 2 + 1, tile % 2 * LANES:(tile % 2 + 1) * LANES]
        layer = long_ref[0, tile] + skip * sig_ref[0, tile]
        layer_ref[:, lanes] = (in_ref[0, tile].astype(F32) * layer).astype(BF16)
        total = long_ref[1, tile] + skip * sig_ref[1, tile]
        kgrad_ref[:, lanes] = (total * in_ref[2, tile].astype(F32)).astype(BF16)
        vgrad_ref[:, lanes] = (total * in_ref[1, tile].astype(F32)).astype(BF16)


PAD = ROWS
HALF = SHARDS // 2


def prepare_filter(land_ref, rows_ref, slide_ref, slid_ref, grad_ref, turn_ref):
    rows_ref[...] = land_ref[...].astype(F32)
    for half in range(2):
        lanes = slice(half * LANES, (half + 1) * LANES)
        for group in range(GROUPS):
            conv_rows = rows_ref[pl.ds(half * 8 + group, SHARDS, stride=16), :]
            for early in range(4):
                slide_ref[early, half, pl.ds(group + 4 * early, SHARDS, stride=4), :] = conv_rows
            grad_ref[half, pl.ds(group, SHARDS, stride=4), :] = rows_ref[
                pl.ds(half * 8 + 4 + group, SHARDS, stride=16), :
            ]
        for early in range(4):
            slid_ref[early, PAD:, lanes] = slide_ref[early, half, :ROWS, :].astype(BF16)
        turn_ref[lanes, :] = lax.dot_general(
            identity(LANES), grad_ref[half].astype(BF16), ACROSS, preferred_element_type=F32
        ).astype(BF16)


def lag_product(block_lag, slid_ref, turn_ref):
    start = PAD - 16 * (block_lag // 4)
    if not isinstance(start, int):
        start = pl.multiple_of(start, 16)
    window = slid_ref[block_lag % 4, pl.ds(start, ROWS), :]
    return jnp.dot(turn_ref[...], window, preferred_element_type=F32)


def lag_rows(prod, corner, later):
    row, lane = iota((LANES, LANES), 0), iota((LANES, LANES), 1)
    causal = (lane == 0) | (row + lane >= LANES)

    def sheared(block):
        block = pltpu.roll(block, 0, 1, stride=1, stride_axis=0)
        return jnp.sum(block.reshape(LANES // SUBS, SUBS, LANES), axis=0)

    odd = prod[LANES:, :LANES] + corner
    even = prod[:LANES, :LANES] + prod[LANES:, LANES:]
    pair = (sheared(jnp.where(causal, even, odd)), sheared(jnp.where(causal, odd, later)))
    return pair, prod[:LANES, LANES:], even


def correlate_lags(longest, shortest, carried, slid_ref, turn_ref, sums_ref):
    corner, later = carried
    for block_lag in range(longest, shortest - 1, -1):
        pair, corner, later = lag_rows(lag_product(block_lag, slid_ref, turn_ref), corner, later)
        place = block_lag * 2 * SUBS
        sums_ref[place:place + SUBS, :] = pair[0]
        sums_ref[place + SUBS:place + 2 * SUBS, :] = pair[1]

    out = []
    count = longest - shortest + 1
    for part in range(2):
        total = None
        for sub in range(SUBS):
            start = (shortest * 2 + part) * SUBS + sub
            rows = sums_ref[pl.ds(start, count, stride=2 * SUBS), :]
            total = rows if total is None else total + rows
        out.append(total)
    return out, (corner, later)


def no_carry():
    return (jnp.zeros((LANES, LANES), F32),) * 2


def seq_copy(src, dst, send, recv, to):
    return pltpu.make_async_remote_copy(
        src_ref=src, dst_ref=dst, send_sem=send, recv_sem=recv,
        device_id={"seq": to}, device_id_type=pl.DeviceIdType.MESH,
    )


def settle(ref, sem):
    pltpu.make_async_copy(ref, ref, sem).wait()


STATES, TOTALS, ENTERING, SHARE, FINAL = 4, 5, 6, 7, 10


def layer_kernel(q_ref, k_ref, v_ref, o_ref, small_ref,
                 layer_ref, kgrad_ref, vgrad_ref, taps_ref,
                 in_ref, sig_ref, spread_ref, pack_ref, land_ref, base_ref, gain_ref, leave_ref, hop_ref, ends_ref,
                 state_ref, left_ref, got_ref, whole_ref, wholes_ref, enter_ref, given_ref, entered_ref, first_ref,
                 long_ref, rows_ref, slide_ref, slid_ref, grad_ref, turn_ref, sums_ref,
                 sent_ref, came_ref, final_ref, home_ref, send_sem, recv_sem, own_sem, in_sem):
    seq, chan = lax.axis_index("seq"), lax.axis_index("chan")
    row, worker = lax.div(seq, WORKERS), lax.rem(seq, WORKERS)
    rates_ref, weights_ref, skip_ref = small_ref.at[:MODES], small_ref.at[MODES:2 * MODES], small_ref.at[2 * MODES:]
    early_pair = lax.div(lax.rem(chan + 1, 4), 2)
    pairs = (early_pair, 1 - early_pair)

    for wave, pair in enumerate(pairs):
        for group in range(GROUPS):
            tile = 2 * group + pair
            for at, source in enumerate((q_ref, k_ref, v_ref, o_ref)):
                pltpu.make_async_copy(
                    source.at[:, pl.ds(pl.multiple_of(tile * LANES, LANES), LANES)],
                    in_ref.at[at, tile], in_sem.at[wave],
                ).start()

    def load_pair(wave):
        settle(in_ref.at[pl.ds(0, 2)], in_sem.at[wave])
        for group in range(GROUPS):
            load_signals(2 * group + pairs[wave], in_ref, sig_ref)

    barrier = pltpu.get_barrier_semaphore()

    def greet(step, _):
        pl.semaphore_signal(barrier, inc=1, device_id={"seq": lax.rem(seq + step, SHARDS)}, device_id_type=pl.DeviceIdType.MESH)
        return _
    lax.fori_loop(1, SHARDS, greet, 0)
    for step in range(1, 4):
        pl.semaphore_signal(barrier, inc=1, device_id={"chan": lax.rem(chan + step, 4)}, device_id_type=pl.DeviceIdType.MESH)

    own_copies = {}

    def send_filter(place):
        mine = pl.ds(pl.multiple_of(seq * 16, 16), 16)
        own = pltpu.make_async_copy(pack_ref.at[place, mine], land_ref.at[place, mine], own_sem.at[place])
        own.start()
        own_copies[place] = own

        def one(step, _):
            to = lax.rem(seq + step, SHARDS)
            seq_copy(
                pack_ref.at[place, pl.ds(pl.multiple_of(to * 16, 16), 16)], land_ref.at[place, mine],
                send_sem.at[place], recv_sem.at[place], to,
            ).start()
            return _
        lax.fori_loop(1, SHARDS, one, 0)

    def to_row(source, target, sem):
        own = pltpu.make_async_copy(source.at[worker], target.at[worker], own_sem.at[sem])
        own.start()

        def one(step, _):
            to = lax.rem(worker + step, WORKERS)
            seq_copy(source.at[to], target.at[worker], send_sem.at[sem], recv_sem.at[sem], row * WORKERS + to).start()
            return _
        lax.fori_loop(1, WORKERS, one, 0)
        return own

    def settle_row(source, target, sem, own):
        own.wait()
        settle(source.at[pl.ds(0, WORKERS - 1)], send_sem.at[sem])
        settle(target.at[pl.ds(0, WORKERS - 1)], recv_sem.at[sem])

    def prepare(place):
        own_copies[place].wait()
        settle(pack_ref.at[place, pl.ds(0, (SHARDS - 1) * 16)], send_sem.at[place])
        settle(land_ref.at[place, pl.ds(0, (SHARDS - 1) * 16)], recv_sem.at[place])
        prepare_filter(land_ref.at[place], rows_ref, slide_ref, slid_ref, grad_ref, turn_ref)

    def share_copy(place):
        return pltpu.make_async_remote_copy(
            src_ref=sent_ref.at[place], dst_ref=came_ref.at[place],
            send_sem=send_sem.at[SHARE + place], recv_sem=recv_sem.at[SHARE + place],
            device_id={"chan": lax.rem(chan + 1 + place, 4)}, device_id_type=pl.DeviceIdType.MESH,
        )

    def correlate_and_share(place):
        prepare(place)
        parts, _ = correlate_lags(SHARDS - 1, 0, no_carry(), slid_ref, turn_ref, sums_ref)
        sent_ref[place] = jnp.concatenate(parts, axis=0).astype(BF16)
        share_copy(place).start()

    make_decays(rates_ref, weights_ref, base_ref, gain_ref, leave_ref, hop_ref)
    slide_ref[...] = jnp.zeros_like(slide_ref)
    slid_ref[:, :PAD, :] = jnp.zeros_like(slid_ref[:, :PAD, :])

    load_pair(0)
    pack_pair(early_pair, chan, sig_ref, spread_ref, pack_ref)
    pl.semaphore_wait(barrier, SHARDS - 1 + 3)
    send_filter(0)

    load_pair(1)
    block_states(sig_ref, base_ref, leave_ref, ends_ref, state_ref, left_ref)
    own_states = to_row(left_ref, got_ref, STATES)
    pack_pair(1 - early_pair, chan, sig_ref, spread_ref, pack_ref)
    send_filter(1)

    settle_row(left_ref, got_ref, STATES, own_states)
    tile_row = iota((TILES, LANES), 0)
    mode_rates = rates_ref[pl.ds(worker, 1), :]
    rate = jnp.where(
        lax.rem(tile_row, 2) == 0,
        jnp.broadcast_to(mode_rates[:, :LANES], (TILES, LANES)),
        jnp.broadcast_to(mode_rates[:, LANES:], (TILES, LANES)),
    )
    decay = jnp.exp(-float(ROWS) * rate)
    zero = jnp.zeros((TILES, LANES), F32)
    fore, back = owner_scan(decay, got_ref, (zero, zero), None)
    whole_ref[:TILES] = fore
    whole_ref[TILES:] = back
    for step in range(1, 4):
        to = lax.rem(row + step, 4)
        seq_copy(
            whole_ref, wholes_ref.at[row], send_sem.at[TOTALS], recv_sem.at[TOTALS], to * WORKERS + worker
        ).start()
    wholes_ref[row] = whole_ref[...]

    correlate_and_share(0)

    for step in range(1, 4):
        settle(whole_ref, send_sem.at[TOTALS])
    settle(wholes_ref.at[pl.ds(0, 3)], recv_sem.at[TOTALS])
    fore, back = zero, zero
    for other in range(4):
        ahead = (row - 1 - other).astype(F32)
        behind = (other - 1 - row).astype(F32)
        length = float(ROWS * WORKERS)
        fore = fore + jnp.where(
            ahead >= 0.0, jnp.exp(-rate * (length * jnp.maximum(ahead, 0.0))), 0.0
        ) * wholes_ref[other, :TILES, :]
        back = back + jnp.where(
            behind >= 0.0, jnp.exp(-rate * (length * jnp.maximum(behind, 0.0))), 0.0
        ) * wholes_ref[other, TILES:, :]
    owner_scan(decay, got_ref, (fore, back), enter_ref)
    given_ref[...] = enter_ref[...].astype(BF16)
    own_entering = to_row(given_ref, entered_ref, ENTERING)
    send_filter(2)
    send_filter(3)

    correlate_and_share(1)

    settle_row(given_ref, entered_ref, ENTERING, own_entering)
    state_ref[...] = entered_ref[...].astype(F32).reshape(MODES * MODES, LANES)
    for place in range(2 * TILES):
        first_ref[place] = state_ref[pl.ds(place, MODES, stride=2 * TILES), :]
    run_recurrence(sig_ref, base_ref, gain_ref, hop_ref, ends_ref, first_ref, long_ref)
    finish_outputs(in_ref, skip_ref, sig_ref, long_ref, layer_ref, kgrad_ref, vgrad_ref)

    correlate_and_share(2)
    prepare(3)
    carried = no_carry()
    for upper in (1, 0):
        low = upper * HALF
        parts, carried = correlate_lags(low + HALF - 1, low, carried, slid_ref, turn_ref, sums_ref)
        if upper:
            for place in range(3):
                share_copy(place).wait()
        for part in range(2):
            rows = slice(part * SHARDS + low, part * SHARDS + low + HALF)
            shares = came_ref[0, rows, :].astype(F32) + came_ref[1, rows, :].astype(F32) + came_ref[2, rows, :].astype(F32)
            final_ref[low:low + HALF, part, :] = parts[part] + shares

        def leave(step, _):
            to = low + lax.rem(seq + step, HALF)

            @pl.when(to != seq)
            def _send():
                seq_copy(final_ref.at[to], home_ref.at[seq], send_sem.at[FINAL], recv_sem.at[FINAL], to).start()
            return _
        lax.fori_loop(0, HALF, leave, 0)
    home_ref[seq] = final_ref[seq]
    settle(final_ref.at[pl.ds(0, SHARDS - 1)], send_sem.at[FINAL])
    settle(home_ref.at[pl.ds(0, SHARDS - 1)], recv_sem.at[FINAL])
    scale = 1.0 / math.sqrt(SEQ_LEN * (CHANNELS // FILTERS))
    for part in range(2):
        taps_ref[:, part * LANES:(part + 1) * LANES] = home_ref[:, part, :] * scale


def hand_on(*refs):
    sources, targets, sem = refs[:4], refs[4:8], refs[8]
    pieces = []
    for at, source in enumerate(sources):
        count = 4 if at < 3 else 1
        rows = source.shape[0] // count
        for piece in range(count):
            some = pl.ds(piece * rows, rows)
            pieces.append(pltpu.make_async_copy(source.at[some], targets[at].at[some], sem.at[at * 4 + piece]))
    for copy in pieces:
        copy.start()
    for copy in pieces:
        copy.wait()


SCRATCH = [
    pltpu.VMEM((4, TILES, ROWS, LANES), BF16),
    pltpu.VMEM((2, TILES, ROWS, LANES), F32),
    pltpu.VMEM((2, SHARDS * 16, LANES), F32),
    pltpu.VMEM((4, SHARDS * 16, LANES), BF16),
    pltpu.VMEM((4, SHARDS * 16, LANES), BF16),
    pltpu.VMEM((2, MODES, SUBS, LANES), F32),
    pltpu.VMEM((2, MODES, SUBS, LANES), F32),
    pltpu.VMEM((2, 2, MODES, SUBS, LANES), F32),
    pltpu.VMEM((2, 2, 3, MODES, SUBS, LANES), F32),
    pltpu.VMEM((2, TILES, MODES, SUBS, LANES), F32),
    pltpu.VMEM((2 * TILES * MODES, LANES), F32),
    pltpu.VMEM((WORKERS, 2 * TILES, LANES), BF16),
    pltpu.VMEM((WORKERS, 2 * TILES, LANES), BF16),
    pltpu.VMEM((2 * TILES, LANES), F32),
    pltpu.VMEM((4, 2 * TILES, LANES), F32),
    pltpu.VMEM((WORKERS, 2 * TILES, LANES), F32),
    pltpu.VMEM((WORKERS, 2 * TILES, LANES), BF16),
    pltpu.VMEM((WORKERS, 2 * TILES, LANES), BF16),
    pltpu.VMEM((2 * TILES, MODES, LANES), F32),
    pltpu.VMEM((2, TILES, ROWS, LANES), F32),
    pltpu.VMEM((SHARDS * 16, LANES), F32),
    pltpu.VMEM((4, 2, ROWS + 16, LANES), F32),
    pltpu.VMEM((4, 2 * ROWS, ROWS), BF16),
    pltpu.VMEM((2, ROWS, LANES), F32),
    pltpu.VMEM((ROWS, ROWS), BF16),
    pltpu.VMEM((SHARDS * 2 * SUBS, LANES), F32),
    pltpu.VMEM((3, LANES, LANES), BF16),
    pltpu.VMEM((3, LANES, LANES), BF16),
    pltpu.VMEM((SHARDS, 2, LANES), F32),
    pltpu.VMEM((SHARDS, 2, LANES), F32),
    pltpu.SemaphoreType.DMA((11,)),
    pltpu.SemaphoreType.DMA((11,)),
    pltpu.SemaphoreType.DMA((11,)),
    pltpu.SemaphoreType.DMA((2,)),
]
VMEM = pl.BlockSpec(memory_space=pltpu.VMEM)


ANY = pl.BlockSpec(memory_space=pl.ANY)


def per_device(query_proj, key_proj, value_proj, out_grad, residues, decay_rate, skip_gain):
    sds = jax.ShapeDtypeStruct
    shapes = (sds((ROWS, 1024), BF16),) * 3 + (sds((SHARDS, ROWS), F32),)
    small = jnp.concatenate([decay_rate.T, residues.T, skip_gain.reshape(4, FILTERS)], axis=0)
    results = pl.pallas_call(
        layer_kernel,
        out_shape=shapes,
        in_specs=[ANY] * 4 + [VMEM],
        out_specs=(VMEM,) * 4,
        scratch_shapes=SCRATCH,
        compiler_params=pltpu.CompilerParams(
            vmem_limit_bytes=53120 * 2**10, collective_id=0, has_side_effects=True
        ),
    )(query_proj, key_proj, value_proj, out_grad, small)
    layer, kgrad, vgrad, taps = pl.pallas_call(
        hand_on,
        out_shape=shapes,
        in_specs=[pl.BlockSpec(memory_space=pltpu.VMEM)] * 4,
        out_specs=(pl.BlockSpec(memory_space=pltpu.HBM),) * 4,
        scratch_shapes=[pltpu.SemaphoreType.DMA((16,))],
        compiler_params=pltpu.CompilerParams(vmem_limit_bytes=53120 * 2**10),
    )(*results)
    return (layer, kgrad, vgrad, taps.T)


def solution(mesh):
    wide = P("seq", "chan")
    return jax.shard_map(
        per_device,
        mesh=mesh,
        in_specs=(wide, wide, wide, wide, P(), P(), P("chan")),
        out_specs=(wide, wide, wide, wide),
        check_vma=False,
    )
```
